32 devices in a mesh: section: 4 (over x, core), fsdp: 8 (over z, y).
Axes of the slice: x: 2, y: 2, z: 4, core: 2. Of those that a mesh axis runs over, the one named last changes fastest.
Arguments:
- signals: bfloat16 [2048, 1536], P('fsdp', 'section'), may hold values from -6 to 6
- conv_weight: bfloat16 [768, 9, 1536], P('fsdp', None, 'section'), may hold values from -0.078125 to 0.078125
- buckets: int32 [2, 2], replicated, may hold values from 0 to 8, as said below
Outputs:
- results: bfloat16 [2048, 1536], P('fsdp', 'section')
- grad_weight: float32 [768, 9, 1536], P('fsdp', None, 'section')
The draws below stay inside these ranges and needn't reach their ends.
Inputs may be any that keep to these rules, and one draw needn't show every extreme that they name: `buckets`: a bucket b means 16 + 2 b live pixels along that side, in the top left of each sample's grid; microbatch 0 has a height bucket of 5 or more; some entry is 8.
All inputs are finite; a program needn't handle non-finite values.
Results may differ from the reference program's by a relative error of at most 0.0054.
Values may be sent and summed in bfloat16 or wider, within the bound.
A program may use at most 128 MiB of HBM per device.

```python
import jax
import jax.numpy as jnp
from jax import lax

C = 768
GROUPS = 32
SIDE = 32
MICRO = 2
TOK_DEV = 256
TOKENS = 2048


def draw_buckets(key, part):
    base = jax.random.fold_in(key, 7)
    key_h, key_first, key_w, key_forced = jax.random.split(base, 4)
    heights = jax.random.randint(key_h, (MICRO,), 0, 9).astype(jnp.int32)
    first_height = jax.random.randint(key_first, (MICRO,), 5, 9).astype(jnp.int32)
    heights = jnp.where(jnp.arange(MICRO) == 0, first_height, heights)
    widths = jax.random.randint(key_w, (MICRO,), 0, 9).astype(jnp.int32)
    table = jnp.stack([heights, widths], axis=1).reshape(2 * MICRO)
    forced = jax.random.randint(key_forced, (1,), 0, 2 * MICRO).astype(jnp.int32)
    table = jnp.where(jnp.arange(2 * MICRO) == forced[0], jnp.full((2 * MICRO,), 8, jnp.int32), table)
    return table.reshape(MICRO, 2).astype(jnp.int32)


def block_scale(key, shape, cuts, least, largest):
    level, own = 1.0, jax.random.fold_in(key, 6)
    for axis_at, shards_of in cuts:
        steps = jnp.exp(jax.random.uniform(jax.random.fold_in(own, axis_at), (shards_of,), jnp.float32, least / len(cuts), largest / len(cuts)))
        level = level * jnp.repeat(steps, shape[axis_at] // shards_of).reshape([-1 if axis == axis_at else 1 for axis in range(len(shape))])
    return level


def normal_values(own_key, extent, scale, bound, cuts=(), dtype=jnp.bfloat16):
    loudness = block_scale(own_key, extent, cuts, -0.22, 0.18) if cuts else 1.0
    result = jax.random.normal(own_key, extent, jnp.float32) * scale * loudness
    return jnp.minimum(jnp.maximum(result, -bound), bound).astype(dtype)


def setup_inputs(seed: int = 0) -> dict:
    splits = jax.random.split(jax.random.key(seed), 4)
    signals = normal_values(splits[0], (TOKENS, 2 * C), 1.0, 6.0, ((0, 8), (1, 4)))
    conv_weight = normal_values(splits[1], (C, 9, 2 * C), (9 * C) ** -0.5, 0.078125, ((0, 8), (2, 4)))
    buckets = draw_buckets(jax.random.fold_in(splits[3], 71), 0)
    return dict(signals=signals, conv_weight=conv_weight, buckets=buckets)


eps = 1e-05

def silu_slope(value):
    sig = jax.nn.sigmoid(value)
    return sig * (1.0 + value * (1.0 - sig))

def group_view(values):
    return values.reshape(values.shape[0], SIDE, SIDE, GROUPS, C // GROUPS)

def pad_grid(field):
    return jnp.pad(field, ((0, 0), (1, 1), (1, 1), (0, 0)))

def convolve(padded, weight):
    samples = padded.shape[0]
    total = jnp.zeros((samples * SIDE * SIDE, weight.shape[-1]), jnp.float32)
    for tap in range(9):
        row_off, col_off = (tap // 3, tap % 3)
        slab = padded[:, row_off:row_off + SIDE, col_off:col_off + SIDE, :].reshape(-1, padded.shape[-1])
        total = total + jnp.dot(slab, weight[:, tap, :], preferred_element_type=jnp.float32)
    return total.reshape(samples, SIDE, SIDE, -1)

def convolve_back(padded, weight):
    samples = padded.shape[0]
    total = jnp.zeros((samples * SIDE * SIDE, weight.shape[0]), jnp.float32)
    for tap in range(9):
        row_off, col_off = (tap // 3, tap % 3)
        slab = padded[:, 2 - row_off:2 - row_off + SIDE, 2 - col_off:2 - col_off + SIDE, :].reshape(-1, padded.shape[-1])
        total = total + lax.dot_general(slab, weight[:, tap, :], (((1,), (1,)), ((), ())), preferred_element_type=jnp.float32)
    return total.reshape(samples, SIDE, SIDE, -1)

def weight_slope(padded, slope):
    flat = slope.reshape(-1, slope.shape[-1])
    taps = []
    for tap in range(9):
        row_off, col_off = (tap // 3, tap % 3)
        slab = padded[:, row_off:row_off + SIDE, col_off:col_off + SIDE, :].reshape(-1, padded.shape[-1])
        taps.append(lax.dot_general(slab, flat, (((0,), (0,)), ((), ())), preferred_element_type=jnp.float32))
    return jnp.stack(taps, axis=1)

def normalize(values, mask, count):
    grouped = group_view(values * mask)
    kcount = (count * (C // GROUPS))[:, None]
    mean = lax.optimization_barrier(jnp.sum(grouped, axis=(1, 2, 4))) / kcount
    spread = lax.optimization_barrier(jnp.sum(grouped * grouped, axis=(1, 2, 4))) / kcount - mean * mean
    scale = lax.rsqrt(spread + eps)
    normed = (group_view(values) - mean[:, None, None, :, None]) * scale[:, None, None, :, None]
    return (normed.reshape(values.shape), scale)

def block_forward(inputs, weight, mask, count):
    values = inputs.astype(jnp.float32)
    normed, scale = normalize(values, mask, count)
    activated = (mask * jax.nn.silu(normed)).astype(jnp.bfloat16)
    padded = pad_grid(activated)
    mixed = convolve(padded, weight)
    output = (values + mask * mixed).astype(jnp.bfloat16)
    return (output, (normed, scale, padded))

def block_backward(grads, cache, weight, mask, count):
    normed, scale, padded = cache
    slope = (grads.astype(jnp.float32) * mask).astype(jnp.bfloat16)
    slope_pad = pad_grid(slope)
    half = C // 2
    upstream = jnp.zeros(normed.shape, jnp.float32)
    for part in range(2):
        partial_value = convolve_back(slope_pad[..., part * half:(part + 1) * half], weight[:, :, part * half:(part + 1) * half])
        upstream = upstream + lax.optimization_barrier(partial_value.astype(jnp.bfloat16)).astype(jnp.float32)
    gated = mask * upstream * silu_slope(normed)
    grouped = group_view(gated)
    normed_grouped = group_view(normed)
    kcount = (count * (C // GROUPS))[:, None]
    first = lax.optimization_barrier(jnp.sum(grouped, axis=(1, 2, 4))) / kcount
    second = lax.optimization_barrier(jnp.sum(grouped * normed_grouped, axis=(1, 2, 4))) / kcount
    centred = grouped - first[:, None, None, :, None] - normed_grouped * second[:, None, None, :, None]
    through = mask * (scale[:, None, None, :, None] * centred).reshape(normed.shape)
    grad_w = weight_slope(padded, slope)
    return (grads.astype(jnp.float32) + through, grad_w)

def reference(signals, conv_weight, buckets):
    samples = TOKENS // (SIDE * SIDE)
    pixels = jnp.roll(signals, TOK_DEV, axis=0)
    grid = pixels.reshape(samples, SIDE, SIDE, 2 * C)
    per_micro = samples // MICRO
    micro_of = (jnp.arange(samples) // per_micro).astype(jnp.int32)
    live_h = 16 + 2 * buckets[micro_of, 0]
    live_w = 16 + 2 * buckets[micro_of, 1]
    cells = jnp.arange(SIDE)
    inside = (cells[None, :, None] < live_h[:, None, None]) & (cells[None, None, :] < live_w[:, None, None])
    mask = inside.astype(jnp.float32)[..., None]
    count = (live_h * live_w).astype(jnp.float32)
    start = (grid[..., :C].astype(jnp.float32) * mask).astype(jnp.bfloat16)
    cotangent = grid[..., C:]
    w_down = conv_weight[:, :, :C]
    w_up = conv_weight[:, :, C:]
    hidden, cache_down = block_forward(start, w_down, mask, count)
    output, cache_up = block_forward(hidden, w_up, mask, count)
    up_grads, grad_up = block_backward(cotangent, cache_up, w_up, mask, count)
    returned = up_grads.astype(jnp.bfloat16)
    down_grads, grad_down = block_backward(returned, cache_down, w_down, mask, count)
    input_grad = (mask * down_grads).astype(jnp.bfloat16)
    results = jnp.concatenate([input_grad, output], axis=-1).reshape(TOKENS, 2 * C)
    results = jnp.roll(results, -TOK_DEV, axis=0)
    grad_weight = jnp.concatenate([grad_down, grad_up], axis=-1)
    return (results, grad_weight)
```

```python
import functools

import jax
import jax.numpy as jnp
from jax import lax
from jax.experimental import pallas as pl
from jax.experimental.pallas import tpu as pltpu
from jax.sharding import PartitionSpec as P

GROUPS = 32
SIDE = 32
MICRO = 2
ROWS_DEV = 8


eps = 1e-05


def from_partner(value, axis, stride):
    mask = 2**stride
    pairs = [(source, source ^ mask) for source in range(lax.axis_size(axis))]
    return lax.ppermute(value, axis, pairs)


def padded_2(cells, sides, width):
    for axis, dim in sides:
        count = lax.axis_size(axis)
        head = lax.slice_in_dim(cells, 0, width, axis=dim)
        tail = lax.slice_in_dim(cells, cells.shape[dim] - width, cells.shape[dim], axis=dim)
        cells = jnp.concatenate(
            [
                lax.ppermute(tail, axis, [(i, (i + 1) % count) for i in range(count)]),
                cells,
                lax.ppermute(head, axis, [((i + 1) % count, i) for i in range(count)]),
            ],
            axis=dim,
        )
    return cells


def silu_slope(value):
    sig = jax.nn.sigmoid(value)
    return sig * (1.0 + value * (1.0 - sig))


def section_swap(value, bit):
    return from_partner(value, "section", bit)


def general(signals, conv_weight, buckets):
    tok = signals.shape[0]
    half = signals.shape[1]
    width = 2 * half
    group_width = width // GROUPS
    local_groups = half // group_width
    section_index = lax.axis_index("section")
    upper_half = section_index % 2 == 1
    role_up = section_index >= 2
    fsdp_index = lax.axis_index("fsdp")
    pieces = SIDE // ROWS_DEV
    samples = lax.axis_size("fsdp") // pieces
    shifted = fsdp_index + 1
    sample_id = shifted // pieces % samples
    piece_id = shifted % pieces
    micro_id = sample_id // (samples // MICRO)
    picked_micro = jnp.arange(MICRO) == micro_id
    bucket_h = jnp.sum(jnp.where(picked_micro, buckets[:, 0], 0))
    bucket_w = jnp.sum(jnp.where(picked_micro, buckets[:, 1], 0))
    live_h = 16 + 2 * bucket_h
    live_w = 16 + 2 * bucket_w
    row_ids = piece_id * ROWS_DEV + jnp.arange(ROWS_DEV)
    col_ids = jnp.arange(SIDE)
    mask_grid = ((row_ids[:, None] < live_h) & (col_ids[None, :] < live_w)).astype(jnp.float32)
    mask_flat = mask_grid.reshape(tok, 1)
    group_count = (live_h * live_w).astype(jnp.float32) * group_width
    sample_hot = (jnp.arange(samples) == sample_id).astype(jnp.float32)[:, None]

    def with_rims(field):
        grid = field.reshape(ROWS_DEV, SIDE, field.shape[-1])
        padded = padded_2(grid, (("fsdp", 0),), 1)
        top = jnp.where(piece_id > 0, padded[:1], jnp.zeros_like(padded[:1]))
        bottom = jnp.where(piece_id < pieces - 1, padded[-1:], jnp.zeros_like(padded[-1:]))
        padded = jnp.concatenate([top, padded[1:-1], bottom], axis=0)
        return jnp.pad(padded, ((0, 0), (1, 1), (0, 0)))

    def group_totals(first, second):
        total_first, total_second = lax.psum(
            (sample_hot * first[None, :], sample_hot * second[None, :]), "fsdp"
        )
        return (
            jnp.sum(sample_hot * total_first, axis=0),
            jnp.sum(sample_hot * total_second, axis=0),
        )

    def normalize(values):
        grouped = values.reshape(tok, local_groups, group_width)
        masked = grouped * mask_flat[:, :, None]
        first = jnp.sum(masked, axis=(0, 2))
        second = jnp.sum(masked * masked, axis=(0, 2))
        total_first, total_second = group_totals(first, second)
        mean = total_first / group_count
        spread = total_second / group_count - mean * mean
        scale = lax.rsqrt(spread + eps)
        normed = (grouped - mean[None, :, None]) * scale[None, :, None]
        return (normed.reshape(tok, half), scale)

    def forward(inputs, weights):
        values = inputs.astype(jnp.float32)
        normed, scale = normalize(values)
        activated = (mask_flat * jax.nn.silu(normed)).astype(jnp.bfloat16)
        padded = with_rims(activated)
        partner = section_swap(padded, 0)
        lower = jnp.where(upper_half, partner, padded)
        upper = jnp.where(upper_half, padded, partner)
        full = jnp.concatenate([lower, upper], axis=-1)
        mixed = jnp.zeros((tok, half), jnp.float32)
        for tap in range(9):
            row_off, col_off = (tap // 3, tap % 3)
            slab = full[row_off : row_off + ROWS_DEV, col_off : col_off + SIDE].reshape(tok, width)
            mixed = mixed + jnp.dot(slab, weights[:, tap, :], preferred_element_type=jnp.float32)
        output = (values + mask_flat * mixed).astype(jnp.bfloat16)
        return (output, (normed, scale, full))

    def backward(grads, cache, weights):
        normed, scale, full = cache
        slope = (grads.astype(jnp.float32) * mask_flat).astype(jnp.bfloat16)
        padded = with_rims(slope)
        partial_value = jnp.zeros((tok, width), jnp.float32)
        for tap in range(9):
            row_off, col_off = (tap // 3, tap % 3)
            slab = padded[
                2 - row_off : 2 - row_off + ROWS_DEV, 2 - col_off : 2 - col_off + SIDE
            ].reshape(tok, half)
            partial_value = partial_value + lax.dot_general(
                slab,
                weights[:, tap, :],
                (((1,), (1,)), ((), ())),
                preferred_element_type=jnp.float32,
            )
        keep = jnp.where(upper_half, partial_value[:, half:], partial_value[:, :half])
        send = jnp.where(upper_half, partial_value[:, :half], partial_value[:, half:]).astype(
            jnp.bfloat16
        )
        arrived = section_swap(send, 0)
        kept = lax.optimization_barrier(keep.astype(jnp.bfloat16)).astype(jnp.float32)
        upstream = kept + arrived.astype(jnp.float32)
        gated = mask_flat * upstream * silu_slope(normed)
        grouped = gated.reshape(tok, local_groups, group_width)
        normed_grouped = normed.reshape(tok, local_groups, group_width)
        first = jnp.sum(grouped, axis=(0, 2))
        second = jnp.sum(grouped * normed_grouped, axis=(0, 2))
        total_first, total_second = group_totals(first, second)
        centred = (
            grouped
            - (total_first / group_count)[None, :, None]
            - normed_grouped * (total_second / group_count)[None, :, None]
        )
        through = mask_flat * (scale[None, :, None] * centred).reshape(tok, half)
        return (grads.astype(jnp.float32) + through, slope)

    weights = lax.all_gather(conv_weight, "fsdp", axis=0, tiled=True)
    start = (signals.astype(jnp.float32) * mask_flat).astype(jnp.bfloat16)
    first_out, first_cache = forward(start, weights)
    handed = section_swap(first_out, 1)
    second_out, second_cache = forward(handed, weights)
    back_weights = lax.all_gather(conv_weight, "fsdp", axis=0, tiled=True)
    up_grads, up_slope = backward(signals, second_cache, back_weights)
    returned = section_swap(up_grads.astype(jnp.bfloat16), 1)
    down_grads, down_slope = backward(returned, first_cache, back_weights)
    results = jnp.where(role_up, second_out, (mask_flat * down_grads).astype(jnp.bfloat16))
    chosen_full = jnp.where(role_up, second_cache[2], first_cache[2])
    chosen_slope = jnp.where(role_up, up_slope, down_slope)
    taps = []
    for tap in range(9):
        row_off, col_off = (tap // 3, tap % 3)
        slab = chosen_full[row_off : row_off + ROWS_DEV, col_off : col_off + SIDE].reshape(
            tok, width
        )
        taps.append(
            lax.dot_general(
                slab, chosen_slope, (((0,), (0,)), ((), ())), preferred_element_type=jnp.float32
            )
        )
    grad_weight = lax.psum_scatter(jnp.stack(taps, axis=1), "fsdp", scatter_dimension=0, tiled=True)
    return (results, grad_weight)


MESH = pl.DeviceIdType.MESH


def place():
    section = lax.axis_index("section")
    return section // 2, section % 2, lax.axis_index("fsdp")


def greet(peers):
    barrier = pltpu.get_barrier_semaphore()
    for peer in peers:
        pl.semaphore_signal(barrier, inc=1, device_id=peer, device_id_type=MESH)
    pl.semaphore_wait(barrier, len(peers))


def remote(src, dst, send, recv, peer):
    return pltpu.make_async_remote_copy(
        src_ref=src, dst_ref=dst, send_sem=send, recv_sem=recv, device_id=peer, device_id_type=MESH
    )


def landed(dst, sem):
    pltpu.make_async_copy(dst, dst, sem).wait()


def communicate(body, cid, args, outs, sems):
    return pl.pallas_call(
        body,
        out_shape=[jax.ShapeDtypeStruct(shape, jnp.bfloat16) for shape in outs],
        in_specs=[pl.BlockSpec(memory_space=pl.ANY)] * len(args),
        out_specs=[pl.BlockSpec(memory_space=pl.ANY)] * len(outs),
        scratch_shapes=[pltpu.SemaphoreType.DMA((count,)) for count in sems],
        compiler_params=pltpu.CompilerParams(collective_id=cid, has_side_effects=True),
    )(*args)


def spread_kernel(n, rows_ref, slices_ref, cols_ref, full_ref, send_a, recv_a, send_g, recv_g):
    block, half, f = place()
    parts = n // 2
    piece = (f + 1) % n
    peers = []
    for d in range(1, 2 * n):
        other = (half * n + f + d) % (2 * n)
        peers.append((2 * block + other // n, other % n))
    greet(peers)
    for j0 in range(parts):
        j = (j0 + f) % parts
        to = parts * half + j
        for core in range(2):
            own = jnp.logical_and(to == f, half == core)
            sem = send_a.at[2 * j0 + core]

            @pl.when(jnp.logical_not(own))
            def _():
                remote(
                    slices_ref.at[j], cols_ref.at[piece], sem, recv_a.at[piece], (2 * block + core, to)
                ).start()

            @pl.when(own)
            def _():
                pltpu.make_async_copy(slices_ref.at[j], cols_ref.at[piece], recv_a.at[piece]).start()

    @pl.when(block == 1)
    def _():
        pltpu.make_async_copy(rows_ref, full_ref.at[piece], recv_g.at[piece]).start()
        for d in range(1, n):
            remote(
                rows_ref, full_ref.at[piece], send_g.at[d], recv_g.at[piece], (2 + half, (f + d) % n)
            ).start()

    for j0 in range(parts):
        j = (j0 + f) % parts
        for core in range(2):
            own = jnp.logical_and(parts * half + j == f, half == core)

            @pl.when(jnp.logical_not(own))
            def _():
                pltpu.make_async_copy(slices_ref.at[j], slices_ref.at[j], send_a.at[2 * j0 + core]).wait()

    for p in range(n):
        landed(cols_ref.at[p], recv_a.at[p])

    @pl.when(block == 1)
    def _():
        for d in range(1, n):
            pltpu.make_async_copy(rows_ref, rows_ref, send_g.at[d]).wait()
        for p in range(n):
            landed(full_ref.at[p], recv_g.at[p])


def reduce_kernel(n, role, mixed_ref, term_ref, parts_ref, other_ref, send, recv, send_t, recv_t):
    block, half, f = place()

    @pl.when(block == role)
    def _():
        greet([(2 * block + half, (f + d) % n) for d in range(1, n)])
        own = pltpu.make_async_copy(mixed_ref.at[(f + 1) % n], parts_ref.at[0], recv.at[0])
        own.start()
        copies = []
        for d in range(1, n):
            to = (f + d) % n
            copies.append(
                remote(
                    mixed_ref.at[(to + 1) % n],
                    parts_ref.at[d],
                    send.at[d],
                    recv.at[d],
                    (2 * block + half, to),
                )
            )
            copies[-1].start()
        own.wait()
        for copy in copies:
            copy.wait()

    @pl.when(block != role)
    def _():
        partner = (2 * block + 1 - half, f)
        greet([partner])
        copy = remote(term_ref, other_ref, send_t.at[0], recv_t.at[0], partner)
        copy.start()
        copy.wait()


def hand_kernel(n, slices_ref, rows_ref, cols_ref, own_ref, send, recv):
    block, half, f = place()
    parts = n // 2
    piece = (f + 1) % n

    @pl.when(block == 0)
    def _():
        greet(
            [(2 + core, parts * half + j) for j in range(parts) for core in range(2)] + [(2 + half, f)]
        )
        copies = []
        for j0 in range(parts):
            j = (j0 + f) % parts
            for core in range(2):
                copies.append(
                    remote(
                        slices_ref.at[j],
                        cols_ref.at[piece],
                        send.at[2 * j0 + core],
                        recv.at[piece],
                        (2 + core, parts * half + j),
                    )
                )
        copies.append(remote(rows_ref, own_ref, send.at[n], recv.at[n], (2 + half, f)))
        for copy in copies:
            copy.start()
        for copy in copies:
            copy.wait_send()

    @pl.when(block == 1)
    def _():
        greet([(f // parts, i) for i in range(n)] + [(half, f)])
        for p in range(n):
            landed(cols_ref.at[p], recv.at[p])
        landed(own_ref, recv.at[n])


def return_kernel(n, grads_ref, full_ref, cols_ref, send, recv):
    block, half, f = place()
    parts = n // 2

    @pl.when(block == 1)
    def _():
        greet([(f // parts, i) for i in range(n)] + [(0, f), (1, f)])
        copies = []
        for d in range(n):
            copies.append(
                remote(
                    grads_ref.at[half],
                    full_ref.at[f % parts, half],
                    send.at[d],
                    recv.at[2 * (f % parts) + half],
                    (f // parts, (f + d) % n),
                )
            )
        for core in range(2):
            copies.append(
                remote(
                    grads_ref.at[half],
                    cols_ref.at[half],
                    send.at[n + core],
                    recv.at[n + half],
                    (core, f),
                )
            )
        for copy in copies:
            copy.start()
        for copy in copies:
            copy.wait_send()

    @pl.when(block == 0)
    def _():
        greet(
            [(2 + core, parts * half + j) for j in range(parts) for core in range(2)]
            + [(2, f), (3, f)]
        )
        for j in range(parts):
            for core in range(2):
                landed(full_ref.at[j, core], recv.at[2 * j + core])
        for core in range(2):
            landed(cols_ref.at[core], recv.at[n + core])


def collect_kernel(n, grads_ref, out_ref, send, recv):
    block, half, f = place()
    parts = n // 2

    @pl.when(block == 0)
    def _():
        greet(
            [((half * n + f + d) % (2 * n) // n, (half * n + f + d) % (2 * n) % n) for d in range(1, 2 * n)]
        )
        mine = f % parts
        for q0 in range(parts):
            piece = half * parts + (q0 + f) % parts
            to = (piece + n - 1) % n
            own = jnp.logical_and(to == f, half == f // parts)

            @pl.when(jnp.logical_not(own))
            def _():
                remote(
                    grads_ref.at[piece], out_ref.at[mine], send.at[q0], recv.at[mine], (f // parts, to)
                ).start()

            @pl.when(own)
            def _():
                pltpu.make_async_copy(grads_ref.at[piece], out_ref.at[mine], recv.at[mine]).start()

        for q0 in range(parts):
            piece = half * parts + (q0 + f) % parts
            own = jnp.logical_and((piece + n - 1) % n == f, half == f // parts)

            @pl.when(jnp.logical_not(own))
            def _():
                pltpu.make_async_copy(grads_ref.at[piece], grads_ref.at[piece], send.at[q0]).wait()

        for j in range(parts):
            landed(out_ref.at[j], recv.at[j])


def channel_split(signals, conv_weight, buckets):
    n = lax.axis_size("fsdp")
    tok, half = signals.shape
    chan = conv_weight.shape[0]
    parts = half // chan
    total = n * tok
    area = SIDE * SIDE
    samples = total // area
    group_width = 2 * half // GROUPS
    section = lax.axis_index("section")
    role_up = section >= 2
    f = lax.axis_index("fsdp")
    piece = (f + 1) % n
    bf16, f32 = jnp.bfloat16, jnp.float32

    live_h = jnp.repeat(16 + 2 * buckets[:, 0], samples // MICRO)
    live_w = jnp.repeat(16 + 2 * buckets[:, 1], samples // MICRO)
    cells = jnp.arange(SIDE)
    inside = (cells[None, :, None] < live_h[:, None, None]) & (cells[None, None, :] < live_w[:, None, None])
    mask = inside.astype(f32).reshape(samples, area, 1)
    mask_own = lax.dynamic_slice_in_dim(mask.reshape(total, 1), piece * tok, tok, axis=0)
    kcount = (live_h * live_w).astype(f32) * group_width

    def group_mean(value):
        columns = jnp.sum(value, axis=1)
        groups = jnp.sum(columns.reshape(samples, chan // group_width, group_width), axis=-1)
        return jnp.repeat(groups / kcount[:, None], group_width, axis=-1)[:, None, :]

    def normalize(values):
        masked = values * mask
        mean = group_mean(masked)
        spread = group_mean(masked * masked) - mean * mean
        scale = lax.rsqrt(spread + eps)
        normed = (values - mean) * scale
        return normed, scale, (mask * jax.nn.silu(normed)).astype(bf16)

    def convolve(active):
        return lax.conv_general_dilated(
            active.reshape(samples, SIDE, SIDE, chan),
            conv_weight.transpose(1, 0, 2).reshape(3, 3, chan, half),
            (1, 1),
            "SAME",
            dimension_numbers=("NHWC", "HWIO", "NHWC"),
            preferred_element_type=f32,
        ).reshape(n, tok, half)

    def convolve_back(slope):
        return (
            lax.conv_general_dilated(
                slope.reshape(samples, SIDE, SIDE, half),
                conv_weight[:, ::-1, :].transpose(1, 2, 0).reshape(3, 3, half, chan),
                (1, 1),
                "SAME",
                dimension_numbers=("NHWC", "HWIO", "NHWC"),
                preferred_element_type=f32,
            )
            .reshape(samples, area, chan)
            .astype(bf16)
        )

    def weight_slope(active, slope):
        grid = jnp.pad(active.reshape(samples, SIDE, SIDE, chan), ((0, 0), (1, 1), (1, 1), (0, 0)))
        flat = slope.reshape(total, half)
        taps = []
        for tap in range(9):
            r, c = tap // 3, tap % 3
            slab = grid[:, r : r + SIDE, c : c + SIDE].reshape(total, chan)
            taps.append(lax.dot_general(slab, flat, (((0,), (0,)), ((), ())), preferred_element_type=f32))
        return jnp.stack(taps, axis=1)

    def input_slope(term, other, normed, scale, grads):
        upstream = term.astype(f32) + other.astype(f32)
        gated = mask * upstream * silu_slope(normed)
        first = group_mean(gated)
        second = group_mean(gated * normed)
        return grads.astype(f32) + mask * (scale * (gated - first - normed * second))

    def sliced(rows):
        return rows.reshape(tok, parts, chan).transpose(1, 0, 2)

    whole = (samples, area, chan)
    cols, full = communicate(
        functools.partial(spread_kernel, n),
        0,
        (signals, sliced(signals)),
        [(n, tok, chan), (n, tok, half)],
        (n, n, n, n),
    )
    cols = cols.reshape(whole)

    def first_down():
        values = (cols.astype(f32) * mask).astype(bf16).astype(f32)
        _, _, active = normalize(values)
        return convolve(active).astype(bf16), jnp.zeros(whole, bf16)

    def first_up():
        slope = (full.reshape(samples, area, half).astype(f32) * mask).astype(bf16)
        return jnp.zeros((n, tok, half), bf16), convolve_back(slope)

    mixed, term = lax.cond(role_up, first_up, first_down)
    partial_rows, other = communicate(
        functools.partial(reduce_kernel, n, 0),
        1,
        (mixed, term),
        [(n, tok, half), whole],
        (n, n, 1, 1),
    )

    def block_rows(rows, pieces):
        return (rows + mask_own * jnp.sum(pieces.astype(f32), axis=0)).astype(bf16)

    start_rows = (signals.astype(f32) * mask_own).astype(bf16).astype(f32)
    handed = block_rows(start_rows, partial_rows)
    skip_cols, skip_rows = communicate(
        functools.partial(hand_kernel, n),
        2,
        (sliced(handed), handed),
        [(n, tok, chan), (tok, half)],
        (n + 1, n + 1),
    )

    def second_up():
        normed, scale, active = normalize(skip_cols.reshape(whole).astype(f32))
        return input_slope(term, other, normed, scale, cols).astype(bf16), active

    def second_down():
        return jnp.zeros(whole, bf16), jnp.zeros(whole, bf16)

    grads, active_up = lax.cond(role_up, second_up, second_down)
    back, back_cols = communicate(
        functools.partial(return_kernel, n),
        3,
        (grads.reshape(2, total // 2, chan),),
        [(parts, 2, total // 2, chan), (2, total // 2, chan)],
        (n + 2, n + 2),
    )

    def third_up():
        slope = (full.reshape(samples, area, half).astype(f32) * mask).astype(bf16)
        mixed = convolve(active_up).astype(bf16)
        return mixed, jnp.zeros(whole, bf16), weight_slope(active_up, slope)

    def third_down():
        joined = back.reshape(parts, total, chan).transpose(1, 0, 2).reshape(samples, area, half)
        slope = (joined.astype(f32) * mask).astype(bf16)
        values = (cols.astype(f32) * mask).astype(bf16).astype(f32)
        _, _, active = normalize(values)
        return jnp.zeros((n, tok, half), bf16), convolve_back(slope), weight_slope(active, slope)

    mixed, term, grad_weight = lax.cond(role_up, third_up, third_down)
    partial_rows, other = communicate(
        functools.partial(reduce_kernel, n, 1),
        4,
        (mixed, term),
        [(n, tok, half), whole],
        (n, n, 1, 1),
    )

    def last_down():
        values = (cols.astype(f32) * mask).astype(bf16).astype(f32)
        normed, scale, _ = normalize(values)
        return (mask * input_slope(term, other, normed, scale, back_cols.reshape(whole))).astype(bf16)

    def last_up():
        return jnp.zeros(whole, bf16)

    grads = lax.cond(role_up, last_up, last_down)
    (pieces,) = communicate(
        functools.partial(collect_kernel, n),
        5,
        (grads.reshape(n, tok, chan),),
        [(parts, tok, chan)],
        (parts, parts),
    )
    down_rows = pieces.transpose(1, 0, 2).reshape(tok, half)
    results = jnp.where(role_up, block_rows(skip_rows.astype(f32), partial_rows), down_rows)
    return results, grad_weight


def per_device(signals, conv_weight, buckets):
    n = lax.axis_size("fsdp")
    chan = conv_weight.shape[0]
    half = signals.shape[1]
    fits = (
        lax.axis_size("section") == 4
        and n % 2 == 0
        and chan % (2 * half // GROUPS) == 0
        and half == chan * (n // 2)
        and n * signals.shape[0] == MICRO * SIDE * SIDE
    )
    return (channel_split if fits else general)(signals, conv_weight, buckets)


def solution(mesh):
    return jax.shard_map(
        per_device,
        mesh=mesh,
        in_specs=(P("fsdp", "section"), P("fsdp", None, "section"), P()),
        out_specs=(P("fsdp", "section"), P("fsdp", None, "section")),
        check_vma=False,
    )
```

```python
import functools

import jax
import jax.numpy as jnp
from jax import lax
from jax.experimental import pallas as pl
from jax.experimental.pallas import tpu as pltpu
from jax.sharding import PartitionSpec as P

GROUPS = 32
SIDE = 32
MICRO = 2
ROWS_DEV = 8


eps = 1e-05


def from_partner(value, axis, stride):
    mask = 2**stride
    pairs = [(source, source ^ mask) for source in range(lax.axis_size(axis))]
    return lax.ppermute(value, axis, pairs)


def padded_2(cells, sides, width):
    for axis, dim in sides:
        count = lax.axis_size(axis)
        head = lax.slice_in_dim(cells, 0, width, axis=dim)
        tail = lax.slice_in_dim(cells, cells.shape[dim] - width, cells.shape[dim], axis=dim)
        cells = jnp.concatenate(
            [
                lax.ppermute(tail, axis, [(i, (i + 1) % count) for i in range(count)]),
                cells,
                lax.ppermute(head, axis, [((i + 1) % count, i) for i in range(count)]),
            ],
            axis=dim,
        )
    return cells


def silu_slope(value):
    sig = jax.nn.sigmoid(value)
    return sig * (1.0 + value * (1.0 - sig))


def section_swap(value, bit):
    return from_partner(value, "section", bit)


def general(signals, conv_weight, buckets):
    tok = signals.shape[0]
    half = signals.shape[1]
    width = 2 * half
    group_width = width // GROUPS
    local_groups = half // group_width
    section_index = lax.axis_index("section")
    upper_half = section_index % 2 == 1
    role_up = section_index >= 2
    fsdp_index = lax.axis_index("fsdp")
    pieces = SIDE // ROWS_DEV
    samples = lax.axis_size("fsdp") // pieces
    shifted = fsdp_index + 1
    sample_id = shifted // pieces % samples
    piece_id = shifted % pieces
    micro_id = sample_id // (samples // MICRO)
    picked_micro = jnp.arange(MICRO) == micro_id
    bucket_h = jnp.sum(jnp.where(picked_micro, buckets[:, 0], 0))
    bucket_w = jnp.sum(jnp.where(picked_micro, buckets[:, 1], 0))
    live_h = 16 + 2 * bucket_h
    live_w = 16 + 2 * bucket_w
    row_ids = piece_id * ROWS_DEV + jnp.arange(ROWS_DEV)
    col_ids = jnp.arange(SIDE)
    mask_grid = ((row_ids[:, None] < live_h) & (col_ids[None, :] < live_w)).astype(jnp.float32)
    mask_flat = mask_grid.reshape(tok, 1)
    group_count = (live_h * live_w).astype(jnp.float32) * group_width
    sample_hot = (jnp.arange(samples) == sample_id).astype(jnp.float32)[:, None]

    def with_rims(field):
        grid = field.reshape(ROWS_DEV, SIDE, field.shape[-1])
        padded = padded_2(grid, (("fsdp", 0),), 1)
        top = jnp.where(piece_id > 0, padded[:1], jnp.zeros_like(padded[:1]))
        bottom = jnp.where(piece_id < pieces - 1, padded[-1:], jnp.zeros_like(padded[-1:]))
        padded = jnp.concatenate([top, padded[1:-1], bottom], axis=0)
        return jnp.pad(padded, ((0, 0), (1, 1), (0, 0)))

    def group_totals(first, second):
        total_first, total_second = lax.psum(
            (sample_hot * first[None, :], sample_hot * second[None, :]), "fsdp"
        )
        return (
            jnp.sum(sample_hot * total_first, axis=0),
            jnp.sum(sample_hot * total_second, axis=0),
        )

    def normalize(values):
        grouped = values.reshape(tok, local_groups, group_width)
        masked = grouped * mask_flat[:, :, None]
        first = jnp.sum(masked, axis=(0, 2))
        second = jnp.sum(masked * masked, axis=(0, 2))
        total_first, total_second = group_totals(first, second)
        mean = total_first / group_count
        spread = total_second / group_count - mean * mean
        scale = lax.rsqrt(spread + eps)
        normed = (grouped - mean[None, :, None]) * scale[None, :, None]
        return (normed.reshape(tok, half), scale)

    def forward(inputs, weights):
        values = inputs.astype(jnp.float32)
        normed, scale = normalize(values)
        activated = (mask_flat * jax.nn.silu(normed)).astype(jnp.bfloat16)
        padded = with_rims(activated)
        partner = section_swap(padded, 0)
        lower = jnp.where(upper_half, partner, padded)
        upper = jnp.where(upper_half, padded, partner)
        full = jnp.concatenate([lower, upper], axis=-1)
        mixed = jnp.zeros((tok, half), jnp.float32)
        for tap in range(9):
            row_off, col_off = (tap // 3, tap % 3)
            slab = full[row_off : row_off + ROWS_DEV, col_off : col_off + SIDE].reshape(tok, width)
            mixed = mixed + jnp.dot(slab, weights[:, tap, :], preferred_element_type=jnp.float32)
        output = (values + mask_flat * mixed).astype(jnp.bfloat16)
        return (output, (normed, scale, full))

    def backward(grads, cache, weights):
        normed, scale, full = cache
        slope = (grads.astype(jnp.float32) * mask_flat).astype(jnp.bfloat16)
        padded = with_rims(slope)
        partial_value = jnp.zeros((tok, width), jnp.float32)
        for tap in range(9):
            row_off, col_off = (tap // 3, tap % 3)
            slab = padded[
                2 - row_off : 2 - row_off + ROWS_DEV, 2 - col_off : 2 - col_off + SIDE
            ].reshape(tok, half)
            partial_value = partial_value + lax.dot_general(
                slab,
                weights[:, tap, :],
                (((1,), (1,)), ((), ())),
                preferred_element_type=jnp.float32,
            )
        keep = jnp.where(upper_half, partial_value[:, half:], partial_value[:, :half])
        send = jnp.where(upper_half, partial_value[:, :half], partial_value[:, half:]).astype(
            jnp.bfloat16
        )
        arrived = section_swap(send, 0)
        kept = lax.optimization_barrier(keep.astype(jnp.bfloat16)).astype(jnp.float32)
        upstream = kept + arrived.astype(jnp.float32)
        gated = mask_flat * upstream * silu_slope(normed)
        grouped = gated.reshape(tok, local_groups, group_width)
        normed_grouped = normed.reshape(tok, local_groups, group_width)
        first = jnp.sum(grouped, axis=(0, 2))
        second = jnp.sum(grouped * normed_grouped, axis=(0, 2))
        total_first, total_second = group_totals(first, second)
        centred = (
            grouped
            - (total_first / group_count)[None, :, None]
            - normed_grouped * (total_second / group_count)[None, :, None]
        )
        through = mask_flat * (scale[None, :, None] * centred).reshape(tok, half)
        return (grads.astype(jnp.float32) + through, slope)

    weights = lax.all_gather(conv_weight, "fsdp", axis=0, tiled=True)
    start = (signals.astype(jnp.float32) * mask_flat).astype(jnp.bfloat16)
    first_out, first_cache = forward(start, weights)
    handed = section_swap(first_out, 1)
    second_out, second_cache = forward(handed, weights)
    back_weights = lax.all_gather(conv_weight, "fsdp", axis=0, tiled=True)
    up_grads, up_slope = backward(signals, second_cache, back_weights)
    returned = section_swap(up_grads.astype(jnp.bfloat16), 1)
    down_grads, down_slope = backward(returned, first_cache, back_weights)
    results = jnp.where(role_up, second_out, (mask_flat * down_grads).astype(jnp.bfloat16))
    chosen_full = jnp.where(role_up, second_cache[2], first_cache[2])
    chosen_slope = jnp.where(role_up, up_slope, down_slope)
    taps = []
    for tap in range(9):
        row_off, col_off = (tap // 3, tap % 3)
        slab = chosen_full[row_off : row_off + ROWS_DEV, col_off : col_off + SIDE].reshape(
            tok, width
        )
        taps.append(
            lax.dot_general(
                slab, chosen_slope, (((0,), (0,)), ((), ())), preferred_element_type=jnp.float32
            )
        )
    grad_weight = lax.psum_scatter(jnp.stack(taps, axis=1), "fsdp", scatter_dimension=0, tiled=True)
    return (results, grad_weight)


MESH = pl.DeviceIdType.MESH


def place():
    section = lax.axis_index("section")
    return section // 2, section % 2, lax.axis_index("fsdp")


def greet(peers):
    barrier = pltpu.get_barrier_semaphore()
    for peer in peers:
        pl.semaphore_signal(barrier, inc=1, device_id=peer, device_id_type=MESH)
    pl.semaphore_wait(barrier, len(peers))


def remote(src, dst, send, recv, peer):
    return pltpu.make_async_remote_copy(
        src_ref=src, dst_ref=dst, send_sem=send, recv_sem=recv, device_id=peer, device_id_type=MESH
    )


def landed(dst, sem):
    pltpu.make_async_copy(dst, dst, sem).wait()


def communicate(body, cid, args, outs, sems):
    return pl.pallas_call(
        body,
        out_shape=[jax.ShapeDtypeStruct(shape, jnp.bfloat16) for shape in outs],
        in_specs=[pl.BlockSpec(memory_space=pl.ANY)] * len(args),
        out_specs=[pl.BlockSpec(memory_space=pl.ANY)] * len(outs),
        scratch_shapes=[pltpu.SemaphoreType.DMA((count,)) for count in sems],
        compiler_params=pltpu.CompilerParams(collective_id=cid, has_side_effects=True),
    )(*args)


def across(f):
    return f + 1 - 2 * (f % 2)


def spread_kernel(n, rows_ref, slices_ref, cols_ref, full_ref, send_a, send_f, recv_a, send_g, recv_g):
    block, half, f = place()
    parts = n // 2
    piece = (f + 1) % n
    peers = []
    for d in range(1, 2 * n):
        other = (half * n + f + d) % (2 * n)
        peers.append((2 * block + other // n, other % n))
    greet(peers)
    for j0 in range(parts):
        j = (j0 + f) % parts
        to = parts * half + j

        @pl.when(to != f)
        def _():
            remote(
                slices_ref.at[j], cols_ref.at[piece], send_a.at[j0], recv_a.at[piece], (2 * block + half, to)
            ).start()

        @pl.when(to == f)
        def _():
            pltpu.make_async_copy(slices_ref.at[j], cols_ref.at[piece], recv_a.at[piece]).start()

    @pl.when(block == 1)
    def _():
        pltpu.make_async_copy(rows_ref, full_ref.at[piece], recv_g.at[piece]).start()
        for d in range(2, n, 2):
            remote(
                rows_ref, full_ref.at[piece], send_g.at[d], recv_g.at[piece], (2 + half, (f + d) % n)
            ).start()
        remote(rows_ref, full_ref.at[piece], send_g.at[0], recv_g.at[piece], (2 + half, across(f))).start()

    @pl.when(half == f // parts)
    def _():
        for p0 in range(n):
            p = (piece + p0) % n
            landed(cols_ref.at[p], recv_a.at[p])
            remote(
                cols_ref.at[p], cols_ref.at[p], send_f.at[p0], recv_a.at[p], (2 * block + 1 - half, f)
            ).start()
        for p0 in range(n):
            p = (piece + p0) % n
            pltpu.make_async_copy(cols_ref.at[p], cols_ref.at[p], send_f.at[p0]).wait()

    @pl.when(half != f // parts)
    def _():
        for p in range(n):
            landed(cols_ref.at[p], recv_a.at[p])

    for j0 in range(parts):
        j = (j0 + f) % parts

        @pl.when(parts * half + j != f)
        def _():
            pltpu.make_async_copy(slices_ref.at[j], slices_ref.at[j], send_a.at[j0]).wait()

    @pl.when(block == 1)
    def _():
        for d in range(2, n, 2):
            p = (piece + d) % n
            landed(full_ref.at[p], recv_g.at[p])
            remote(
                full_ref.at[p], full_ref.at[p], send_g.at[d + 1], recv_g.at[p], (2 + half, across(f))
            ).start()
        for d in range(0, n, 2):
            pltpu.make_async_copy(rows_ref, rows_ref, send_g.at[d]).wait()
        for d in range(2, n, 2):
            p = (piece + d) % n
            pltpu.make_async_copy(full_ref.at[p], full_ref.at[p], send_g.at[d + 1]).wait()
        landed(full_ref.at[piece], recv_g.at[piece])
        for d in range(0, n, 2):
            p = (across(f) + 1 + d) % n
            landed(full_ref.at[p], recv_g.at[p])


def reduce_kernel(n, role, mixed_ref, term_ref, parts_ref, other_ref, send, recv, send_t, recv_t):
    block, half, f = place()

    @pl.when(block == role)
    def _():
        greet([(2 * block + half, (f + d) % n) for d in range(1, n)])
        own = pltpu.make_async_copy(mixed_ref.at[(f + 1) % n], parts_ref.at[0], recv.at[0])
        own.start()
        copies = []
        for d in range(1, n):
            to = (f + d) % n
            copies.append(
                remote(
                    mixed_ref.at[(to + 1) % n],
                    parts_ref.at[d],
                    send.at[d],
                    recv.at[d],
                    (2 * block + half, to),
                )
            )
            copies[-1].start()
        own.wait()
        for copy in copies:
            copy.wait()

    @pl.when(block != role)
    def _():
        partner = (2 * block + 1 - half, f)
        greet([partner])
        copy = remote(term_ref, other_ref, send_t.at[0], recv_t.at[0], partner)
        copy.start()
        copy.wait()


def hand_kernel(n, slices_ref, rows_ref, cols_ref, own_ref, send, recv, send_f):
    block, half, f = place()
    parts = n // 2
    piece = (f + 1) % n

    @pl.when(block == 0)
    def _():
        greet([(2 + half, parts * half + j) for j in range(parts)] + [(2 + half, f)])
        copies = []
        for j0 in range(parts):
            j = (j0 + f) % parts
            copies.append(
                remote(
                    slices_ref.at[j],
                    cols_ref.at[piece],
                    send.at[j0],
                    recv.at[piece],
                    (2 + half, parts * half + j),
                )
            )
        copies.append(remote(rows_ref, own_ref, send.at[n], recv.at[n], (2 + half, f)))
        for copy in copies:
            copy.start()
        for copy in copies:
            copy.wait_send()

    @pl.when(jnp.logical_and(block == 1, half == f // parts))
    def _():
        greet([(half, i) for i in range(n)] + [(half, f), (3 - half, f)])
        for p0 in range(n):
            p = (piece + p0) % n
            landed(cols_ref.at[p], recv.at[p])
            remote(cols_ref.at[p], cols_ref.at[p], send_f.at[p0], recv.at[p], (3 - half, f)).start()
        for p0 in range(n):
            p = (piece + p0) % n
            pltpu.make_async_copy(cols_ref.at[p], cols_ref.at[p], send_f.at[p0]).wait()
        landed(own_ref, recv.at[n])

    @pl.when(jnp.logical_and(block == 1, half != f // parts))
    def _():
        greet([(half, f), (3 - half, f)])
        for p in range(n):
            landed(cols_ref.at[p], recv.at[p])
        landed(own_ref, recv.at[n])


def return_kernel(n, grads_ref, full_ref, cols_ref, send, recv, send_f):
    block, half, f = place()
    parts = n // 2

    @pl.when(block == 1)
    def _():
        line = [(f // parts, (f + d) % n) for d in range(0, n, 2)]
        greet(line + [(0, f), (1, f)])
        copies = []
        for i, peer in enumerate(line):
            copies.append(
                remote(
                    grads_ref.at[half],
                    full_ref.at[f % parts, half],
                    send.at[i],
                    recv.at[2 * (f % parts) + half],
                    peer,
                )
            )
        for core in range(2):
            copies.append(
                remote(
                    grads_ref.at[half],
                    cols_ref.at[half],
                    send.at[n + core],
                    recv.at[n + half],
                    (core, f),
                )
            )
        for copy in copies:
            copy.start()
        for copy in copies:
            copy.wait_send()

    @pl.when(block == 0)
    def _():
        near = [f % 2 + j for j in range(0, parts, 2)]
        far = [1 - f % 2 + j for j in range(0, parts, 2)]
        greet(
            [(2 + core, parts * half + j) for j in near for core in range(2)]
            + [(2, f), (3, f), (half, across(f))]
        )
        copies = []
        for i, j in enumerate(near):
            for core in range(2):
                landed(full_ref.at[j, core], recv.at[2 * j + core])
                copies.append(
                    remote(
                        full_ref.at[j, core],
                        full_ref.at[j, core],
                        send_f.at[2 * i + core],
                        recv.at[2 * j + core],
                        (half, across(f)),
                    )
                )
                copies[-1].start()
        for core in range(2):
            landed(cols_ref.at[core], recv.at[n + core])
        for copy in copies:
            copy.wait_send()
        for j in far:
            for core in range(2):
                landed(full_ref.at[j, core], recv.at[2 * j + core])


def taps_kernel(samples, active_ref, out_ref):
    area = SIDE * SIDE
    lanes = active_ref.shape[1]
    col = lax.broadcasted_iota(jnp.int32, (area, lanes), 0) % SIDE
    for s in range(samples):
        base = s * area
        here = active_ref[base : base + area, :].astype(jnp.float32)
        before = jnp.where(col > 0, pltpu.roll(here, 1, 0), 0.0).astype(jnp.bfloat16)
        after = jnp.where(col < SIDE - 1, pltpu.roll(here, area - 1, 0), 0.0).astype(jnp.bfloat16)
        edge = jnp.zeros((SIDE, lanes), jnp.bfloat16)
        for c, value in enumerate((before, here.astype(jnp.bfloat16), after)):
            up = slice(c * lanes, (c + 1) * lanes)
            mid = slice((3 + c) * lanes, (4 + c) * lanes)
            down = slice((6 + c) * lanes, (7 + c) * lanes)
            out_ref[base + SIDE : base + area, up] = value[: area - SIDE]
            out_ref[base : base + SIDE, up] = edge
            out_ref[base : base + area, mid] = value
            out_ref[base : base + area - SIDE, down] = value[SIDE:]
            out_ref[base + area - SIDE : base + area, down] = edge


def join_kernel(parts, slices_ref, out_ref):
    chan = slices_ref.shape[-1]
    for j in range(parts):
        out_ref[:, j * chan : (j + 1) * chan] = slices_ref[j]


def local(body, out, *args):
    return pl.pallas_call(
        body,
        out_shape=out,
        in_specs=[pl.BlockSpec(memory_space=pltpu.VMEM)] * len(args),
        out_specs=pl.BlockSpec(memory_space=pltpu.VMEM),
        compiler_params=pltpu.CompilerParams(vmem_limit_bytes=40 * 2**20),
    )(*args)


def collect_kernel(n, grads_ref, out_ref, send, recv):
    block, half, f = place()
    parts = n // 2

    @pl.when(block == 0)
    def _():
        greet(
            [((half * n + f + d) % (2 * n) // n, (half * n + f + d) % (2 * n) % n) for d in range(1, 2 * n)]
        )
        mine = f % parts
        for q0 in range(parts):
            piece = half * parts + (q0 + f) % parts
            to = (piece + n - 1) % n
            own = jnp.logical_and(to == f, half == f // parts)

            @pl.when(jnp.logical_not(own))
            def _():
                remote(
                    grads_ref.at[piece], out_ref.at[mine], send.at[q0], recv.at[mine], (f // parts, to)
                ).start()

            @pl.when(own)
            def _():
                pltpu.make_async_copy(grads_ref.at[piece], out_ref.at[mine], recv.at[mine]).start()

        for q0 in range(parts):
            piece = half * parts + (q0 + f) % parts
            own = jnp.logical_and((piece + n - 1) % n == f, half == f // parts)

            @pl.when(jnp.logical_not(own))
            def _():
                pltpu.make_async_copy(grads_ref.at[piece], grads_ref.at[piece], send.at[q0]).wait()

        for j in range(parts):
            landed(out_ref.at[j], recv.at[j])


def channel_split(signals, conv_weight, buckets):
    n = lax.axis_size("fsdp")
    tok, half = signals.shape
    chan = conv_weight.shape[0]
    parts = half // chan
    total = n * tok
    area = SIDE * SIDE
    samples = total // area
    group_width = 2 * half // GROUPS
    section = lax.axis_index("section")
    role_up = section >= 2
    f = lax.axis_index("fsdp")
    piece = (f + 1) % n
    bf16, f32 = jnp.bfloat16, jnp.float32

    live_h = jnp.repeat(16 + 2 * buckets[:, 0], samples // MICRO)
    live_w = jnp.repeat(16 + 2 * buckets[:, 1], samples // MICRO)
    cells = jnp.arange(SIDE)
    inside = (cells[None, :, None] < live_h[:, None, None]) & (cells[None, None, :] < live_w[:, None, None])
    mask = inside.astype(f32).reshape(samples, area, 1)
    mask_own = lax.dynamic_slice_in_dim(mask.reshape(total, 1), piece * tok, tok, axis=0)
    kcount = (live_h * live_w).astype(f32) * group_width

    def group_mean(value):
        columns = jnp.sum(value, axis=1)
        groups = jnp.sum(columns.reshape(samples, chan // group_width, group_width), axis=-1)
        return jnp.repeat(groups / kcount[:, None], group_width, axis=-1)[:, None, :]

    def normalize(values):
        masked = values * mask
        mean = group_mean(masked)
        spread = group_mean(masked * masked) - mean * mean
        scale = lax.rsqrt(spread + eps)
        normed = (values - mean) * scale
        return normed, scale, (mask * jax.nn.silu(normed)).astype(bf16)

    lanes = 128

    def taps_of(active):
        padded = jnp.pad(active.reshape(total, chan), ((0, 0), (0, lanes - chan)))
        return local(
            functools.partial(taps_kernel, samples),
            jax.ShapeDtypeStruct((total, 9 * lanes), bf16),
            padded,
        )

    def convolve(taps):
        weight = jnp.pad(conv_weight.transpose(1, 0, 2), ((0, 0), (0, lanes - chan), (0, 0)))
        return jnp.dot(taps, weight.reshape(9 * lanes, half), preferred_element_type=f32).reshape(n, tok, half)

    def convolve_back(slope):
        return (
            lax.conv_general_dilated(
                slope.reshape(samples, SIDE, SIDE, half),
                conv_weight[:, ::-1, :].transpose(1, 2, 0).reshape(3, 3, half, chan),
                (1, 1),
                "SAME",
                dimension_numbers=("NHWC", "HWIO", "NHWC"),
                preferred_element_type=f32,
            )
            .reshape(samples, area, chan)
            .astype(bf16)
        )

    def weight_slope(taps, slope):
        whole_taps = lax.dot_general(
            taps, slope.reshape(total, half), (((0,), (0,)), ((), ())), preferred_element_type=f32
        )
        return whole_taps.reshape(9, lanes, half)[:, :chan].transpose(1, 0, 2)

    def input_slope(term, other, normed, scale, grads):
        upstream = term.astype(f32) + other.astype(f32)
        gated = mask * upstream * silu_slope(normed)
        first = group_mean(gated)
        second = group_mean(gated * normed)
        return grads.astype(f32) + mask * (scale * (gated - first - normed * second))

    def sliced(rows):
        return rows.reshape(tok, parts, chan).transpose(1, 0, 2)

    whole = (samples, area, chan)
    cols, full = communicate(
        functools.partial(spread_kernel, n),
        0,
        (signals, sliced(signals)),
        [(n, tok, chan), (n, tok, half)],
        (parts, n, n, n, n),
    )
    cols = cols.reshape(whole)

    values = (cols.astype(f32) * mask).astype(bf16).astype(f32)
    normed_down, scale_down, active_down = normalize(values)
    taps_down = taps_of(active_down)

    def first_down():
        return convolve(taps_down).astype(bf16), jnp.zeros(whole, bf16)

    def first_up():
        slope = (full.reshape(samples, area, half).astype(f32) * mask).astype(bf16)
        return jnp.zeros((n, tok, half), bf16), convolve_back(slope)

    mixed, term = lax.cond(role_up, first_up, first_down)
    partial_rows, other = communicate(
        functools.partial(reduce_kernel, n, 0),
        1,
        (mixed, term),
        [(n, tok, half), whole],
        (n, n, 1, 1),
    )

    def block_rows(rows, pieces):
        return (rows + mask_own * jnp.sum(pieces.astype(f32), axis=0)).astype(bf16)

    start_rows = (signals.astype(f32) * mask_own).astype(bf16).astype(f32)
    handed = block_rows(start_rows, partial_rows)
    skip_cols, skip_rows = communicate(
        functools.partial(hand_kernel, n),
        2,
        (sliced(handed), handed),
        [(n, tok, chan), (tok, half)],
        (n + 1, n + 1, n),
    )

    def second_up():
        normed, scale, active = normalize(skip_cols.reshape(whole).astype(f32))
        slope = mask * input_slope(term, other, normed, scale, cols)
        return slope.astype(bf16), active

    def second_down():
        return jnp.zeros(whole, bf16), jnp.zeros(whole, bf16)

    grads, active_up = lax.cond(role_up, second_up, second_down)
    back, back_cols = communicate(
        functools.partial(return_kernel, n),
        3,
        (grads.reshape(2, total // 2, chan),),
        [(parts, 2, total // 2, chan), (2, total // 2, chan)],
        (n + 2, n + 2, n),
    )

    def third_up():
        slope = (full.reshape(samples, area, half).astype(f32) * mask).astype(bf16)
        taps_up = taps_of(active_up)
        return convolve(taps_up).astype(bf16), jnp.zeros(whole, bf16), weight_slope(taps_up, slope)

    def third_down():
        slope = local(
            functools.partial(join_kernel, parts),
            jax.ShapeDtypeStruct((total, half), bf16),
            back.reshape(parts, total, chan),
        )
        return jnp.zeros((n, tok, half), bf16), convolve_back(slope), weight_slope(taps_down, slope)

    mixed, term, grad_weight = lax.cond(role_up, third_up, third_down)
    partial_rows, other = communicate(
        functools.partial(reduce_kernel, n, 1),
        4,
        (mixed, term),
        [(n, tok, half), whole],
        (n, n, 1, 1),
    )

    def last_down():
        slope = input_slope(term, other, normed_down, scale_down, back_cols.reshape(whole))
        return (mask * slope).astype(bf16)

    def last_up():
        return jnp.zeros(whole, bf16)

    grads = lax.cond(role_up, last_up, last_down)
    (pieces,) = communicate(
        functools.partial(collect_kernel, n),
        5,
        (grads.reshape(n, tok, chan),),
        [(parts, tok, chan)],
        (parts, parts),
    )
    down_rows = pieces.transpose(1, 0, 2).reshape(tok, half)
    results = jnp.where(role_up, block_rows(skip_rows.astype(f32), partial_rows), down_rows)
    return results, grad_weight


def per_device(signals, conv_weight, buckets):
    n = lax.axis_size("fsdp")
    chan = conv_weight.shape[0]
    half = signals.shape[1]
    fits = (
        lax.axis_size("section") == 4
        and n % 4 == 0
        and chan <= 128
        and chan % (2 * half // GROUPS) == 0
        and half == chan * (n // 2)
        and n * signals.shape[0] == MICRO * SIDE * SIDE
    )
    return (channel_split if fits else general)(signals, conv_weight, buckets)


def solution(mesh):
    return jax.shard_map(
        per_device,
        mesh=mesh,
        in_specs=(P("fsdp", "section"), P("fsdp", None, "section"), P()),
        out_specs=(P("fsdp", "section"), P("fsdp", None, "section")),
        check_vma=False,
    )
```

```python
import functools

import jax
import jax.numpy as jnp
from jax import lax
from jax.experimental import pallas as pl
from jax.experimental.pallas import tpu as pltpu
from jax.sharding import PartitionSpec as P

GROUPS = 32
SIDE = 32
MICRO = 2
ROWS_DEV = 8


eps = 1e-05


def from_partner(value, axis, stride):
    mask = 2**stride
    pairs = [(source, source ^ mask) for source in range(lax.axis_size(axis))]
    return lax.ppermute(value, axis, pairs)


def padded_2(cells, sides, width):
    for axis, dim in sides:
        count = lax.axis_size(axis)
        head = lax.slice_in_dim(cells, 0, width, axis=dim)
        tail = lax.slice_in_dim(cells, cells.shape[dim] - width, cells.shape[dim], axis=dim)
        cells = jnp.concatenate(
            [
                lax.ppermute(tail, axis, [(i, (i + 1) % count) for i in range(count)]),
                cells,
                lax.ppermute(head, axis, [((i + 1) % count, i) for i in range(count)]),
            ],
            axis=dim,
        )
    return cells


def silu_slope(value):
    sig = jax.nn.sigmoid(value)
    return sig * (1.0 + value * (1.0 - sig))


def section_swap(value, bit):
    return from_partner(value, "section", bit)


def general(signals, conv_weight, buckets):
    tok = signals.shape[0]
    half = signals.shape[1]
    width = 2 * half
    group_width = width // GROUPS
    local_groups = half // group_width
    section_index = lax.axis_index("section")
    upper_half = section_index % 2 == 1
    role_up = section_index >= 2
    fsdp_index = lax.axis_index("fsdp")
    pieces = SIDE // ROWS_DEV
    samples = lax.axis_size("fsdp") // pieces
    shifted = fsdp_index + 1
    sample_id = shifted // pieces % samples
    piece_id = shifted % pieces
    micro_id = sample_id // (samples // MICRO)
    picked_micro = jnp.arange(MICRO) == micro_id
    bucket_h = jnp.sum(jnp.where(picked_micro, buckets[:, 0], 0))
    bucket_w = jnp.sum(jnp.where(picked_micro, buckets[:, 1], 0))
    live_h = 16 + 2 * bucket_h
    live_w = 16 + 2 * bucket_w
    row_ids = piece_id * ROWS_DEV + jnp.arange(ROWS_DEV)
    col_ids = jnp.arange(SIDE)
    mask_grid = ((row_ids[:, None] < live_h) & (col_ids[None, :] < live_w)).astype(jnp.float32)
    mask_flat = mask_grid.reshape(tok, 1)
    group_count = (live_h * live_w).astype(jnp.float32) * group_width
    sample_hot = (jnp.arange(samples) == sample_id).astype(jnp.float32)[:, None]

    def with_rims(field):
        grid = field.reshape(ROWS_DEV, SIDE, field.shape[-1])
        padded = padded_2(grid, (("fsdp", 0),), 1)
        top = jnp.where(piece_id > 0, padded[:1], jnp.zeros_like(padded[:1]))
        bottom = jnp.where(piece_id < pieces - 1, padded[-1:], jnp.zeros_like(padded[-1:]))
        padded = jnp.concatenate([top, padded[1:-1], bottom], axis=0)
        return jnp.pad(padded, ((0, 0), (1, 1), (0, 0)))

    def group_totals(first, second):
        total_first, total_second = lax.psum(
            (sample_hot * first[None, :], sample_hot * second[None, :]), "fsdp"
        )
        return (
            jnp.sum(sample_hot * total_first, axis=0),
            jnp.sum(sample_hot * total_second, axis=0),
        )

    def normalize(values):
        grouped = values.reshape(tok, local_groups, group_width)
        masked = grouped * mask_flat[:, :, None]
        first = jnp.sum(masked, axis=(0, 2))
        second = jnp.sum(masked * masked, axis=(0, 2))
        total_first, total_second = group_totals(first, second)
        mean = total_first / group_count
        spread = total_second / group_count - mean * mean
        scale = lax.rsqrt(spread + eps)
        normed = (grouped - mean[None, :, None]) * scale[None, :, None]
        return (normed.reshape(tok, half), scale)

    def forward(inputs, weights):
        values = inputs.astype(jnp.float32)
        normed, scale = normalize(values)
        activated = (mask_flat * jax.nn.silu(normed)).astype(jnp.bfloat16)
        padded = with_rims(activated)
        partner = section_swap(padded, 0)
        lower = jnp.where(upper_half, partner, padded)
        upper = jnp.where(upper_half, padded, partner)
        full = jnp.concatenate([lower, upper], axis=-1)
        mixed = jnp.zeros((tok, half), jnp.float32)
        for tap in range(9):
            row_off, col_off = (tap // 3, tap % 3)
            slab = full[row_off : row_off + ROWS_DEV, col_off : col_off + SIDE].reshape(tok, width)
            mixed = mixed + jnp.dot(slab, weights[:, tap, :], preferred_element_type=jnp.float32)
        output = (values + mask_flat * mixed).astype(jnp.bfloat16)
        return (output, (normed, scale, full))

    def backward(grads, cache, weights):
        normed, scale, full = cache
        slope = (grads.astype(jnp.float32) * mask_flat).astype(jnp.bfloat16)
        padded = with_rims(slope)
        partial_value = jnp.zeros((tok, width), jnp.float32)
        for tap in range(9):
            row_off, col_off = (tap // 3, tap % 3)
            slab = padded[
                2 - row_off : 2 - row_off + ROWS_DEV, 2 - col_off : 2 - col_off + SIDE
            ].reshape(tok, half)
            partial_value = partial_value + lax.dot_general(
                slab,
                weights[:, tap, :],
                (((1,), (1,)), ((), ())),
                preferred_element_type=jnp.float32,
            )
        keep = jnp.where(upper_half, partial_value[:, half:], partial_value[:, :half])
        send = jnp.where(upper_half, partial_value[:, :half], partial_value[:, half:]).astype(
            jnp.bfloat16
        )
        arrived = section_swap(send, 0)
        kept = lax.optimization_barrier(keep.astype(jnp.bfloat16)).astype(jnp.float32)
        upstream = kept + arrived.astype(jnp.float32)
        gated = mask_flat * upstream * silu_slope(normed)
        grouped = gated.reshape(tok, local_groups, group_width)
        normed_grouped = normed.reshape(tok, local_groups, group_width)
        first = jnp.sum(grouped, axis=(0, 2))
        second = jnp.sum(grouped * normed_grouped, axis=(0, 2))
        total_first, total_second = group_totals(first, second)
        centred = (
            grouped
            - (total_first / group_count)[None, :, None]
            - normed_grouped * (total_second / group_count)[None, :, None]
        )
        through = mask_flat * (scale[None, :, None] * centred).reshape(tok, half)
        return (grads.astype(jnp.float32) + through, slope)

    weights = lax.all_gather(conv_weight, "fsdp", axis=0, tiled=True)
    start = (signals.astype(jnp.float32) * mask_flat).astype(jnp.bfloat16)
    first_out, first_cache = forward(start, weights)
    handed = section_swap(first_out, 1)
    second_out, second_cache = forward(handed, weights)
    back_weights = lax.all_gather(conv_weight, "fsdp", axis=0, tiled=True)
    up_grads, up_slope = backward(signals, second_cache, back_weights)
    returned = section_swap(up_grads.astype(jnp.bfloat16), 1)
    down_grads, down_slope = backward(returned, first_cache, back_weights)
    results = jnp.where(role_up, second_out, (mask_flat * down_grads).astype(jnp.bfloat16))
    chosen_full = jnp.where(role_up, second_cache[2], first_cache[2])
    chosen_slope = jnp.where(role_up, up_slope, down_slope)
    taps = []
    for tap in range(9):
        row_off, col_off = (tap // 3, tap % 3)
        slab = chosen_full[row_off : row_off + ROWS_DEV, col_off : col_off + SIDE].reshape(
            tok, width
        )
        taps.append(
            lax.dot_general(
                slab, chosen_slope, (((0,), (0,)), ((), ())), preferred_element_type=jnp.float32
            )
        )
    grad_weight = lax.psum_scatter(jnp.stack(taps, axis=1), "fsdp", scatter_dimension=0, tiled=True)
    return (results, grad_weight)


MESH = pl.DeviceIdType.MESH


def place():
    section = lax.axis_index("section")
    return section // 2, section % 2, lax.axis_index("fsdp")


def greet(peers):
    barrier = pltpu.get_barrier_semaphore()
    for peer in peers:
        pl.semaphore_signal(barrier, inc=1, device_id=peer, device_id_type=MESH)
    pl.semaphore_wait(barrier, len(peers))


def remote(src, dst, send, recv, peer):
    return pltpu.make_async_remote_copy(
        src_ref=src, dst_ref=dst, send_sem=send, recv_sem=recv, device_id=peer, device_id_type=MESH
    )


def landed(dst, sem):
    pltpu.make_async_copy(dst, dst, sem).wait()


def communicate(body, cid, args, outs, sems, scratch=(), fast=()):
    spaces = [pltpu.VMEM if i in fast else pl.ANY for i in range(len(args) + len(outs))]
    specs = [pl.BlockSpec(memory_space=space) for space in spaces]
    return pl.pallas_call(
        body,
        out_shape=[jax.ShapeDtypeStruct(shape, dtype) for shape, dtype in outs],
        in_specs=specs[: len(args)],
        out_specs=specs[len(args) :],
        scratch_shapes=list(scratch) + [pltpu.SemaphoreType.DMA((count,)) for count in sems],
        compiler_params=pltpu.CompilerParams(
            collective_id=cid, has_side_effects=True, vmem_limit_bytes=40 * 2**20
        ),
    )(*args)


def across(f):
    return f + 1 - 2 * (f % 2)


def spread_kernel(n, rows_ref, slices_ref, cols_ref, full_ref, send_a, send_f, recv_a, send_g, recv_g):
    block, half, f = place()
    parts = n // 2
    piece = (f + 1) % n
    peers = []
    for d in range(1, 2 * n):
        other = (half * n + f + d) % (2 * n)
        peers.append((2 * block + other // n, other % n))
    greet(peers)
    for j0 in range(parts):
        j = (j0 + f) % parts
        to = parts * half + j

        @pl.when(to != f)
        def _():
            remote(
                slices_ref.at[j], cols_ref.at[piece], send_a.at[j0], recv_a.at[piece], (2 * block + half, to)
            ).start()

        @pl.when(to == f)
        def _():
            pltpu.make_async_copy(slices_ref.at[j], cols_ref.at[piece], recv_a.at[piece]).start()

    @pl.when(block == 1)
    def _():
        pltpu.make_async_copy(rows_ref, full_ref.at[piece], recv_g.at[piece]).start()
        for d in range(2, n, 2):
            remote(
                rows_ref, full_ref.at[piece], send_g.at[d], recv_g.at[piece], (2 + half, (f + d) % n)
            ).start()
        remote(rows_ref, full_ref.at[piece], send_g.at[0], recv_g.at[piece], (2 + half, across(f))).start()

    @pl.when(block == 1)
    def _():
        for d in range(2, n, 2):
            p = (piece + d) % n
            landed(full_ref.at[p], recv_g.at[p])
            remote(
                full_ref.at[p], full_ref.at[p], send_g.at[d + 1], recv_g.at[p], (2 + half, across(f))
            ).start()

    @pl.when(half == f // parts)
    def _():
        for p0 in range(n):
            p = (piece + p0) % n
            landed(cols_ref.at[p], recv_a.at[p])
            remote(
                cols_ref.at[p], cols_ref.at[p], send_f.at[p0], recv_a.at[p], (2 * block + 1 - half, f)
            ).start()
        for p0 in range(n):
            p = (piece + p0) % n
            pltpu.make_async_copy(cols_ref.at[p], cols_ref.at[p], send_f.at[p0]).wait()

    @pl.when(half != f // parts)
    def _():
        for p in range(n):
            landed(cols_ref.at[p], recv_a.at[p])

    @pl.when(block == 1)
    def _():
        for d in range(0, n, 2):
            pltpu.make_async_copy(rows_ref, rows_ref, send_g.at[d]).wait()
        for d in range(2, n, 2):
            p = (piece + d) % n
            pltpu.make_async_copy(full_ref.at[p], full_ref.at[p], send_g.at[d + 1]).wait()
        landed(full_ref.at[piece], recv_g.at[piece])
        for d in range(0, n, 2):
            p = (across(f) + 1 + d) % n
            landed(full_ref.at[p], recv_g.at[p])

    for j0 in range(parts):
        j = (j0 + f) % parts

        @pl.when(parts * half + j != f)
        def _():
            pltpu.make_async_copy(slices_ref.at[j], slices_ref.at[j], send_a.at[j0]).wait()


def reduce_kernel(
    n, role, mixed_ref, term_ref, sum_ref, other_ref, near, pair, far, send, recv, send_z, recv_z, send_t, recv_t
):
    block, half, f = place()

    @pl.when(block == role)
    def _():
        section = 2 * block + half
        greet([(section, across(f))] + [(section, (f + d) % n) for d in range(2, n, 2)])
        order = sorted(range(0, n, 2), key=lambda d: -min(d, n - d))
        copies = []
        for d in order:
            to = (across(f) + d) % n
            copies.append(
                remote(
                    mixed_ref.at[(to + 1) % n],
                    near.at[d // 2],
                    send.at[d // 2],
                    recv.at[d // 2],
                    (section, across(f)),
                )
            )
            copies[-1].start()
        onward = []
        for d, copy in zip(order, copies):
            copy.wait_recv()
            both = mixed_ref[(f + d + 1) % n].astype(jnp.float32) + near[d // 2].astype(jnp.float32)
            if d:
                pair[d // 2] = both.astype(jnp.bfloat16)
                onward.append(
                    remote(
                        pair.at[d // 2],
                        far.at[d // 2],
                        send_z.at[d // 2],
                        recv_z.at[d // 2],
                        (section, (f + d) % n),
                    )
                )
                onward[-1].start()
            else:
                sum_ref[...] = both
        for d, copy in zip(order, onward):
            copy.wait_recv()
            sum_ref[...] += far[d // 2].astype(jnp.float32)
        for copy in copies + onward:
            copy.wait_send()

    @pl.when(block != role)
    def _():
        partner = (2 * block + 1 - half, f)
        greet([partner])
        copy = remote(term_ref, other_ref, send_t.at[0], recv_t.at[0], partner)
        copy.start()
        copy.wait()


def hand_kernel(n, slices_ref, rows_ref, cols_ref, own_ref, send, recv, send_f):
    block, half, f = place()
    parts = n // 2
    piece = (f + 1) % n

    @pl.when(block == 0)
    def _():
        greet([(2 + half, parts * half + j) for j in range(parts)] + [(2 + half, f)])
        copies = []
        for j0 in range(parts):
            j = (j0 + f) % parts
            copies.append(
                remote(
                    slices_ref.at[j],
                    cols_ref.at[piece],
                    send.at[j0],
                    recv.at[piece],
                    (2 + half, parts * half + j),
                )
            )
        copies.append(remote(rows_ref, own_ref, send.at[n], recv.at[n], (2 + half, f)))
        for copy in copies:
            copy.start()
        for copy in copies:
            copy.wait_send()

    @pl.when(jnp.logical_and(block == 1, half == f // parts))
    def _():
        greet([(half, i) for i in range(n)] + [(half, f), (3 - half, f)])
        for p0 in range(n):
            p = (piece + p0) % n
            landed(cols_ref.at[p], recv.at[p])
            remote(cols_ref.at[p], cols_ref.at[p], send_f.at[p0], recv.at[p], (3 - half, f)).start()
        for p0 in range(n):
            p = (piece + p0) % n
            pltpu.make_async_copy(cols_ref.at[p], cols_ref.at[p], send_f.at[p0]).wait()
        landed(own_ref, recv.at[n])

    @pl.when(jnp.logical_and(block == 1, half != f // parts))
    def _():
        greet([(half, f), (3 - half, f)])
        for p in range(n):
            landed(cols_ref.at[p], recv.at[p])
        landed(own_ref, recv.at[n])


def return_kernel(n, grads_ref, full_ref, cols_ref, send, recv, send_z, send_f):
    block, half, f = place()
    parts = n // 2

    @pl.when(block == 1)
    def _():
        greet([(0, f), (1, f)])
        copies = [
            remote(
                grads_ref.at[half],
                full_ref.at[half, f % parts],
                send.at[0],
                recv.at[2 * (f % parts) + half],
                (f // parts, f),
            )
        ]
        for core in range(2):
            copies.append(
                remote(
                    grads_ref.at[half],
                    cols_ref.at[half],
                    send.at[1 + core],
                    recv.at[n + half],
                    (core, f),
                )
            )
        for copy in copies:
            copy.start()
        for copy in copies:
            copy.wait_send()

    @pl.when(block == 0)
    def _():
        line = [(half, (f + d) % n) for d in sorted(range(2, n, 2), key=lambda d: -min(d, n - d))]
        greet([(2, f), (3, f), (half, across(f))] + line)
        steps = parts // 2
        near = [f % 2 + 2 * ((i + f // 2) % steps) for i in range(steps)]
        far = [1 - f % 2 + 2 * ((i + f // 2) % steps) for i in range(steps)]
        copies = []
        for i, j in enumerate(near):
            for core in range(2):
                slot = full_ref.at[core, j]
                landed(slot, recv.at[2 * j + core])
                if i == 0:

                    @pl.when(parts * half + j == f)
                    def _():
                        for q, peer in enumerate(line):
                            remote(
                                slot, slot, send_z.at[2 * q + core], recv.at[2 * j + core], peer
                            ).start()

                copies.append(
                    remote(slot, slot, send_f.at[2 * i + core], recv.at[2 * j + core], (half, across(f)))
                )
                copies[-1].start()
        for core in range(2):
            landed(cols_ref.at[core], recv.at[n + core])
        for copy in copies:
            copy.wait_send()

        @pl.when(parts * half + near[0] == f)
        def _():
            for q in range(len(line)):
                for core in range(2):
                    slot = full_ref.at[core, near[0]]
                    pltpu.make_async_copy(slot, slot, send_z.at[2 * q + core]).wait()

        for j in far:
            for core in range(2):
                landed(full_ref.at[core, j], recv.at[2 * j + core])


def taps_kernel(samples, active_ref, out_ref):
    area = SIDE * SIDE
    lanes = active_ref.shape[1]
    col = lax.broadcasted_iota(jnp.int32, (area, lanes), 0) % SIDE
    for s in range(samples):
        base = s * area
        here = active_ref[base : base + area, :].astype(jnp.float32)
        before = jnp.where(col > 0, pltpu.roll(here, 1, 0), 0.0).astype(jnp.bfloat16)
        after = jnp.where(col < SIDE - 1, pltpu.roll(here, area - 1, 0), 0.0).astype(jnp.bfloat16)
        edge = jnp.zeros((SIDE, lanes), jnp.bfloat16)
        for c, value in enumerate((before, here.astype(jnp.bfloat16), after)):
            up = slice(c * lanes, (c + 1) * lanes)
            mid = slice((3 + c) * lanes, (4 + c) * lanes)
            down = slice((6 + c) * lanes, (7 + c) * lanes)
            out_ref[base + SIDE : base + area, up] = value[: area - SIDE]
            out_ref[base : base + SIDE, up] = edge
            out_ref[base : base + area, mid] = value
            out_ref[base : base + area - SIDE, down] = value[SIDE:]
            out_ref[base + area - SIDE : base + area, down] = edge


def local(body, out, *args):
    return pl.pallas_call(
        body,
        out_shape=out,
        in_specs=[pl.BlockSpec(memory_space=pltpu.VMEM)] * len(args),
        out_specs=pl.BlockSpec(memory_space=pltpu.VMEM),
        compiler_params=pltpu.CompilerParams(vmem_limit_bytes=40 * 2**20),
    )(*args)


def collect_kernel(n, grads_ref, out_ref, send, recv):
    block, half, f = place()
    parts = n // 2

    @pl.when(block == 0)
    def _():
        greet(
            [((half * n + f + d) % (2 * n) // n, (half * n + f + d) % (2 * n) % n) for d in range(1, 2 * n)]
        )
        mine = f % parts
        for q0 in range(parts):
            piece = half * parts + (q0 + f) % parts
            to = (piece + n - 1) % n
            own = jnp.logical_and(to == f, half == f // parts)

            @pl.when(jnp.logical_not(own))
            def _():
                remote(
                    grads_ref.at[piece], out_ref.at[mine], send.at[q0], recv.at[mine], (f // parts, to)
                ).start()

            @pl.when(own)
            def _():
                pltpu.make_async_copy(grads_ref.at[piece], out_ref.at[mine], recv.at[mine]).start()

        for q0 in range(parts):
            piece = half * parts + (q0 + f) % parts
            own = jnp.logical_and((piece + n - 1) % n == f, half == f // parts)

            @pl.when(jnp.logical_not(own))
            def _():
                pltpu.make_async_copy(grads_ref.at[piece], grads_ref.at[piece], send.at[q0]).wait()

        for j in range(parts):
            landed(out_ref.at[j], recv.at[j])


def channel_split(signals, conv_weight, buckets):
    n = lax.axis_size("fsdp")
    tok, half = signals.shape
    chan = conv_weight.shape[0]
    parts = half // chan
    total = n * tok
    area = SIDE * SIDE
    samples = total // area
    group_width = 2 * half // GROUPS
    section = lax.axis_index("section")
    role_up = section >= 2
    f = lax.axis_index("fsdp")
    piece = (f + 1) % n
    bf16, f32 = jnp.bfloat16, jnp.float32

    live_h = jnp.repeat(16 + 2 * buckets[:, 0], samples // MICRO)
    live_w = jnp.repeat(16 + 2 * buckets[:, 1], samples // MICRO)
    cells = jnp.arange(SIDE)
    inside = (cells[None, :, None] < live_h[:, None, None]) & (cells[None, None, :] < live_w[:, None, None])
    mask = inside.astype(f32).reshape(samples, area, 1)
    mask_own = lax.dynamic_slice_in_dim(mask.reshape(total, 1), piece * tok, tok, axis=0)
    kcount = (live_h * live_w).astype(f32) * group_width

    def group_mean(value):
        columns = jnp.sum(value, axis=1)
        groups = jnp.sum(columns.reshape(samples, chan // group_width, group_width), axis=-1)
        return jnp.repeat(groups / kcount[:, None], group_width, axis=-1)[:, None, :]

    def normalize(values):
        masked = values * mask
        mean = group_mean(masked)
        spread = group_mean(masked * masked) - mean * mean
        scale = lax.rsqrt(spread + eps)
        normed = (values - mean) * scale
        return normed, scale, (mask * jax.nn.silu(normed)).astype(bf16)

    lanes = 128

    def taps_of(active):
        padded = jnp.pad(active.reshape(total, chan), ((0, 0), (0, lanes - chan)))
        return local(
            functools.partial(taps_kernel, samples),
            jax.ShapeDtypeStruct((total, 9 * lanes), bf16),
            padded,
        )

    def convolve(taps):
        weight = jnp.pad(conv_weight.transpose(1, 0, 2), ((0, 0), (0, lanes - chan), (0, 0)))
        return jnp.dot(taps, weight.reshape(9 * lanes, half), preferred_element_type=f32).reshape(n, tok, half)

    def convolve_back(slope):
        return (
            lax.conv_general_dilated(
                slope.reshape(samples, SIDE, SIDE, half),
                conv_weight[:, ::-1, :].transpose(1, 2, 0).reshape(3, 3, half, chan),
                (1, 1),
                "SAME",
                dimension_numbers=("NHWC", "HWIO", "NHWC"),
                preferred_element_type=f32,
            )
            .reshape(samples, area, chan)
            .astype(bf16)
        )

    def weight_slope(taps, slope):
        whole_taps = lax.dot_general(
            taps, slope.reshape(total, half), (((0,), (0,)), ((), ())), preferred_element_type=f32
        )
        return whole_taps.reshape(9, lanes, half)[:, :chan].transpose(1, 0, 2)

    def input_slope(term, other, normed, scale, grads):
        upstream = term.astype(f32) + other.astype(f32)
        gated = mask * upstream * silu_slope(normed)
        first = group_mean(gated)
        second = group_mean(gated * normed)
        return grads.astype(f32) + mask * (scale * (gated - first - normed * second))

    def sliced(rows):
        return rows.reshape(tok, parts, chan).transpose(1, 0, 2)

    whole = (samples, area, chan)
    cols, full = communicate(
        functools.partial(spread_kernel, n),
        0,
        (signals, sliced(signals)),
        [((n, tok, chan), bf16), ((n, tok, half), bf16)],
        (parts, n, n, n, n),
    )
    cols = cols.reshape(whole)

    values = (cols.astype(f32) * mask).astype(bf16).astype(f32)
    normed_down, scale_down, active_down = normalize(values)
    taps_down = taps_of(active_down)

    def first_down():
        return convolve(taps_down).astype(bf16), jnp.zeros(whole, bf16)

    def first_up():
        slope = (full.reshape(samples, area, half).astype(f32) * mask).astype(bf16)
        return jnp.zeros((n, tok, half), bf16), convolve_back(slope)

    mixed, term = lax.cond(role_up, first_up, first_down)
    partial_rows, other = communicate(
        functools.partial(reduce_kernel, n, 0),
        1,
        (mixed, term),
        [((tok, half), f32), (whole, bf16)],
        (parts, parts, parts, parts, 1, 1),
        [pltpu.VMEM((parts, tok, half), bf16)] * 3,
        (0, 2),
    )

    def block_rows(rows, pieces):
        return (rows + mask_own * pieces).astype(bf16)

    start_rows = (signals.astype(f32) * mask_own).astype(bf16).astype(f32)
    handed = block_rows(start_rows, partial_rows)
    skip_cols, skip_rows = communicate(
        functools.partial(hand_kernel, n),
        2,
        (sliced(handed), handed),
        [((n, tok, chan), bf16), ((tok, half), bf16)],
        (n + 1, n + 1, n),
    )

    def second_up():
        normed, scale, active = normalize(skip_cols.reshape(whole).astype(f32))
        slope = mask * input_slope(term, other, normed, scale, cols)
        return slope.astype(bf16), active

    def second_down():
        return jnp.zeros(whole, bf16), jnp.zeros(whole, bf16)

    grads, active_up = lax.cond(role_up, second_up, second_down)
    back, back_cols = communicate(
        functools.partial(return_kernel, n),
        3,
        (grads.reshape(2, total // 2, chan).transpose(0, 2, 1),),
        [((2, parts, chan, total // 2), bf16), ((2, chan, total // 2), bf16)],
        (3, n + 2, n, parts),
    )

    def third_up():
        slope = (full.reshape(samples, area, half).astype(f32) * mask).astype(bf16)
        taps_up = taps_of(active_up)
        return convolve(taps_up).astype(bf16), jnp.zeros(whole, bf16), weight_slope(taps_up, slope)

    def third_down():
        slope = back.reshape(2, half, total // 2).transpose(0, 2, 1).reshape(total, half)
        return jnp.zeros((n, tok, half), bf16), convolve_back(slope), weight_slope(taps_down, slope)

    mixed, term, grad_weight = lax.cond(role_up, third_up, third_down)
    partial_rows, other = communicate(
        functools.partial(reduce_kernel, n, 1),
        4,
        (mixed, term),
        [((tok, half), f32), (whole, bf16)],
        (parts, parts, parts, parts, 1, 1),
        [pltpu.VMEM((parts, tok, half), bf16)] * 3,
        (0, 2),
    )

    def last_down():
        slope = input_slope(term, other, normed_down, scale_down, back_cols.transpose(0, 2, 1).reshape(whole))
        return (mask * slope).astype(bf16)

    def last_up():
        return jnp.zeros(whole, bf16)

    grads = lax.cond(role_up, last_up, last_down)
    (pieces,) = communicate(
        functools.partial(collect_kernel, n),
        5,
        (grads.reshape(n, tok, chan),),
        [((parts, tok, chan), bf16)],
        (parts, parts),
    )
    down_rows = pieces.transpose(1, 0, 2).reshape(tok, half)
    results = jnp.where(role_up, block_rows(skip_rows.astype(f32), partial_rows), down_rows)
    return results, grad_weight


def per_device(signals, conv_weight, buckets):
    n = lax.axis_size("fsdp")
    chan = conv_weight.shape[0]
    half = signals.shape[1]
    fits = (
        lax.axis_size("section") == 4
        and n % 4 == 0
        and chan <= 128
        and chan % (2 * half // GROUPS) == 0
        and half == chan * (n // 2)
        and n * signals.shape[0] == MICRO * SIDE * SIDE
    )
    return (channel_split if fits else general)(signals, conv_weight, buckets)


def solution(mesh):
    return jax.shard_map(
        per_device,
        mesh=mesh,
        in_specs=(P("fsdp", "section"), P("fsdp", None, "section"), P()),
        out_specs=(P("fsdp", "section"), P("fsdp", None, "section")),
        check_vma=False,
    )
```

```python
import functools

import jax
import jax.numpy as jnp
from jax import lax
from jax.experimental import pallas as pl
from jax.experimental.pallas import tpu as pltpu
from jax.sharding import PartitionSpec as P

GROUPS = 32
SIDE = 32
MICRO = 2
ROWS_DEV = 8


eps = 1e-05


def from_partner(value, axis, stride):
    mask = 2**stride
    pairs = [(source, source ^ mask) for source in range(lax.axis_size(axis))]
    return lax.ppermute(value, axis, pairs)


def padded_2(cells, sides, width):
    for axis, dim in sides:
        count = lax.axis_size(axis)
        head = lax.slice_in_dim(cells, 0, width, axis=dim)
        tail = lax.slice_in_dim(cells, cells.shape[dim] - width, cells.shape[dim], axis=dim)
        cells = jnp.concatenate(
            [
                lax.ppermute(tail, axis, [(i, (i + 1) % count) for i in range(count)]),
                cells,
                lax.ppermute(head, axis, [((i + 1) % count, i) for i in range(count)]),
            ],
            axis=dim,
        )
    return cells


def silu_slope(value):
    sig = jax.nn.sigmoid(value)
    return sig * (1.0 + value * (1.0 - sig))


def section_swap(value, bit):
    return from_partner(value, "section", bit)


def general(signals, conv_weight, buckets):
    tok = signals.shape[0]
    half = signals.shape[1]
    width = 2 * half
    group_width = width // GROUPS
    local_groups = half // group_width
    section_index = lax.axis_index("section")
    upper_half = section_index % 2 == 1
    role_up = section_index >= 2
    fsdp_index = lax.axis_index("fsdp")
    pieces = SIDE // ROWS_DEV
    samples = lax.axis_size("fsdp") // pieces
    shifted = fsdp_index + 1
    sample_id = shifted // pieces % samples
    piece_id = shifted % pieces
    micro_id = sample_id // (samples // MICRO)
    picked_micro = jnp.arange(MICRO) == micro_id
    bucket_h = jnp.sum(jnp.where(picked_micro, buckets[:, 0], 0))
    bucket_w = jnp.sum(jnp.where(picked_micro, buckets[:, 1], 0))
    live_h = 16 + 2 * bucket_h
    live_w = 16 + 2 * bucket_w
    row_ids = piece_id * ROWS_DEV + jnp.arange(ROWS_DEV)
    col_ids = jnp.arange(SIDE)
    mask_grid = ((row_ids[:, None] < live_h) & (col_ids[None, :] < live_w)).astype(jnp.float32)
    mask_flat = mask_grid.reshape(tok, 1)
    group_count = (live_h * live_w).astype(jnp.float32) * group_width
    sample_hot = (jnp.arange(samples) == sample_id).astype(jnp.float32)[:, None]

    def with_rims(field):
        grid = field.reshape(ROWS_DEV, SIDE, field.shape[-1])
        padded = padded_2(grid, (("fsdp", 0),), 1)
        top = jnp.where(piece_id > 0, padded[:1], jnp.zeros_like(padded[:1]))
        bottom = jnp.where(piece_id < pieces - 1, padded[-1:], jnp.zeros_like(padded[-1:]))
        padded = jnp.concatenate([top, padded[1:-1], bottom], axis=0)
        return jnp.pad(padded, ((0, 0), (1, 1), (0, 0)))

    def group_totals(first, second):
        total_first, total_second = lax.psum(
            (sample_hot * first[None, :], sample_hot * second[None, :]), "fsdp"
        )
        return (
            jnp.sum(sample_hot * total_first, axis=0),
            jnp.sum(sample_hot * total_second, axis=0),
        )

    def normalize(values):
        grouped = values.reshape(tok, local_groups, group_width)
        masked = grouped * mask_flat[:, :, None]
        first = jnp.sum(masked, axis=(0, 2))
        second = jnp.sum(masked * masked, axis=(0, 2))
        total_first, total_second = group_totals(first, second)
        mean = total_first / group_count
        spread = total_second / group_count - mean * mean
        scale = lax.rsqrt(spread + eps)
        normed = (grouped - mean[None, :, None]) * scale[None, :, None]
        return (normed.reshape(tok, half), scale)

    def forward(inputs, weights):
        values = inputs.astype(jnp.float32)
        normed, scale = normalize(values)
        activated = (mask_flat * jax.nn.silu(normed)).astype(jnp.bfloat16)
        padded = with_rims(activated)
        partner = section_swap(padded, 0)
        lower = jnp.where(upper_half, partner, padded)
        upper = jnp.where(upper_half, padded, partner)
        full = jnp.concatenate([lower, upper], axis=-1)
        mixed = jnp.zeros((tok, half), jnp.float32)
        for tap in range(9):
            row_off, col_off = (tap // 3, tap % 3)
            slab = full[row_off : row_off + ROWS_DEV, col_off : col_off + SIDE].reshape(tok, width)
            mixed = mixed + jnp.dot(slab, weights[:, tap, :], preferred_element_type=jnp.float32)
        output = (values + mask_flat * mixed).astype(jnp.bfloat16)
        return (output, (normed, scale, full))

    def backward(grads, cache, weights):
        normed, scale, full = cache
        slope = (grads.astype(jnp.float32) * mask_flat).astype(jnp.bfloat16)
        padded = with_rims(slope)
        partial_value = jnp.zeros((tok, width), jnp.float32)
        for tap in range(9):
            row_off, col_off = (tap // 3, tap % 3)
            slab = padded[
                2 - row_off : 2 - row_off + ROWS_DEV, 2 - col_off : 2 - col_off + SIDE
            ].reshape(tok, half)
            partial_value = partial_value + lax.dot_general(
                slab,
                weights[:, tap, :],
                (((1,), (1,)), ((), ())),
                preferred_element_type=jnp.float32,
            )
        keep = jnp.where(upper_half, partial_value[:, half:], partial_value[:, :half])
        send = jnp.where(upper_half, partial_value[:, :half], partial_value[:, half:]).astype(
            jnp.bfloat16
        )
        arrived = section_swap(send, 0)
        kept = lax.optimization_barrier(keep.astype(jnp.bfloat16)).astype(jnp.float32)
        upstream = kept + arrived.astype(jnp.float32)
        gated = mask_flat * upstream * silu_slope(normed)
        grouped = gated.reshape(tok, local_groups, group_width)
        normed_grouped = normed.reshape(tok, local_groups, group_width)
        first = jnp.sum(grouped, axis=(0, 2))
        second = jnp.sum(grouped * normed_grouped, axis=(0, 2))
        total_first, total_second = group_totals(first, second)
        centred = (
            grouped
            - (total_first / group_count)[None, :, None]
            - normed_grouped * (total_second / group_count)[None, :, None]
        )
        through = mask_flat * (scale[None, :, None] * centred).reshape(tok, half)
        return (grads.astype(jnp.float32) + through, slope)

    weights = lax.all_gather(conv_weight, "fsdp", axis=0, tiled=True)
    start = (signals.astype(jnp.float32) * mask_flat).astype(jnp.bfloat16)
    first_out, first_cache = forward(start, weights)
    handed = section_swap(first_out, 1)
    second_out, second_cache = forward(handed, weights)
    back_weights = lax.all_gather(conv_weight, "fsdp", axis=0, tiled=True)
    up_grads, up_slope = backward(signals, second_cache, back_weights)
    returned = section_swap(up_grads.astype(jnp.bfloat16), 1)
    down_grads, down_slope = backward(returned, first_cache, back_weights)
    results = jnp.where(role_up, second_out, (mask_flat * down_grads).astype(jnp.bfloat16))
    chosen_full = jnp.where(role_up, second_cache[2], first_cache[2])
    chosen_slope = jnp.where(role_up, up_slope, down_slope)
    taps = []
    for tap in range(9):
        row_off, col_off = (tap // 3, tap % 3)
        slab = chosen_full[row_off : row_off + ROWS_DEV, col_off : col_off + SIDE].reshape(
            tok, width
        )
        taps.append(
            lax.dot_general(
                slab, chosen_slope, (((0,), (0,)), ((), ())), preferred_element_type=jnp.float32
            )
        )
    grad_weight = lax.psum_scatter(jnp.stack(taps, axis=1), "fsdp", scatter_dimension=0, tiled=True)
    return (results, grad_weight)


MESH = pl.DeviceIdType.MESH


def place():
    section = lax.axis_index("section")
    return section // 2, section % 2, lax.axis_index("fsdp")


def greet(peers):
    barrier = pltpu.get_barrier_semaphore()
    for peer in peers:
        pl.semaphore_signal(barrier, inc=1, device_id=peer, device_id_type=MESH)
    pl.semaphore_wait(barrier, len(peers))


def remote(src, dst, send, recv, peer):
    return pltpu.make_async_remote_copy(
        src_ref=src, dst_ref=dst, send_sem=send, recv_sem=recv, device_id=peer, device_id_type=MESH
    )


def landed(dst, sem):
    pltpu.make_async_copy(dst, dst, sem).wait()


def communicate(body, cid, args, outs, sems, scratch=(), fast=()):
    spaces = [pltpu.VMEM if i in fast else pl.ANY for i in range(len(args) + len(outs))]
    specs = [pl.BlockSpec(memory_space=space) for space in spaces]
    return pl.pallas_call(
        body,
        out_shape=[jax.ShapeDtypeStruct(shape, dtype) for shape, dtype in outs],
        in_specs=specs[: len(args)],
        out_specs=specs[len(args) :],
        scratch_shapes=list(scratch) + [pltpu.SemaphoreType.DMA((count,)) for count in sems],
        compiler_params=pltpu.CompilerParams(
            collective_id=cid, has_side_effects=True, vmem_limit_bytes=40 * 2**20
        ),
    )(*args)


def across(f):
    return f + 1 - 2 * (f % 2)


def spread_kernel(n, rows_ref, slices_ref, cols_ref, full_ref, send_a, send_f, recv_a, send_g, recv_g):
    block, half, f = place()
    parts = n // 2
    piece = (f + 1) % n
    peers = []
    for d in range(1, 2 * n):
        other = (half * n + f + d) % (2 * n)
        peers.append((2 * block + other // n, other % n))
    greet(peers)
    for j0 in range(parts):
        j = (j0 + f) % parts
        to = parts * half + j

        @pl.when(to != f)
        def _():
            remote(
                slices_ref.at[j], cols_ref.at[piece], send_a.at[j0], recv_a.at[piece], (2 * block + half, to)
            ).start()

        @pl.when(to == f)
        def _():
            pltpu.make_async_copy(slices_ref.at[j], cols_ref.at[piece], recv_a.at[piece]).start()

    @pl.when(block == 1)
    def _():
        pltpu.make_async_copy(rows_ref, full_ref.at[piece], recv_g.at[piece]).start()
        for d in range(2, n, 2):
            remote(
                rows_ref, full_ref.at[piece], send_g.at[d], recv_g.at[piece], (2 + half, (f + d) % n)
            ).start()
        remote(rows_ref, full_ref.at[piece], send_g.at[0], recv_g.at[piece], (2 + half, across(f))).start()

    @pl.when(block == 1)
    def _():
        for d in range(2, n, 2):
            p = (piece + d) % n
            landed(full_ref.at[p], recv_g.at[p])
            remote(
                full_ref.at[p], full_ref.at[p], send_g.at[d + 1], recv_g.at[p], (2 + half, across(f))
            ).start()

    @pl.when(half == f // parts)
    def _():
        for p0 in range(n):
            p = (piece + p0) % n
            landed(cols_ref.at[p], recv_a.at[p])
            remote(
                cols_ref.at[p], cols_ref.at[p], send_f.at[p0], recv_a.at[p], (2 * block + 1 - half, f)
            ).start()
        for p0 in range(n):
            p = (piece + p0) % n
            pltpu.make_async_copy(cols_ref.at[p], cols_ref.at[p], send_f.at[p0]).wait()

    @pl.when(half != f // parts)
    def _():
        for p in range(n):
            landed(cols_ref.at[p], recv_a.at[p])

    @pl.when(block == 1)
    def _():
        for d in range(0, n, 2):
            pltpu.make_async_copy(rows_ref, rows_ref, send_g.at[d]).wait()
        for d in range(2, n, 2):
            p = (piece + d) % n
            pltpu.make_async_copy(full_ref.at[p], full_ref.at[p], send_g.at[d + 1]).wait()
        landed(full_ref.at[piece], recv_g.at[piece])
        for d in range(0, n, 2):
            p = (across(f) + 1 + d) % n
            landed(full_ref.at[p], recv_g.at[p])

    for j0 in range(parts):
        j = (j0 + f) % parts

        @pl.when(parts * half + j != f)
        def _():
            pltpu.make_async_copy(slices_ref.at[j], slices_ref.at[j], send_a.at[j0]).wait()


def reduce_kernel(
    n, role, mixed_ref, term_ref, sum_ref, other_ref, near, pair, far, send, recv, send_z, recv_z, send_t, recv_t
):
    block, half, f = place()

    @pl.when(block == role)
    def _():
        section = 2 * block + half
        greet([(section, across(f))] + [(section, (f + d) % n) for d in range(2, n, 2)])
        order = sorted(range(0, n, 2), key=lambda d: -min(d, n - d))
        copies = []
        for d in order:
            to = (across(f) + d) % n
            copies.append(
                remote(
                    mixed_ref.at[(to + 1) % n],
                    near.at[d // 2],
                    send.at[d // 2],
                    recv.at[d // 2],
                    (section, across(f)),
                )
            )
            copies[-1].start()
        onward = []
        for d, copy in zip(order, copies):
            copy.wait_recv()
            both = mixed_ref[(f + d + 1) % n].astype(jnp.float32) + near[d // 2].astype(jnp.float32)
            if d:
                pair[d // 2] = both.astype(jnp.bfloat16)
                onward.append(
                    remote(
                        pair.at[d // 2],
                        far.at[d // 2],
                        send_z.at[d // 2],
                        recv_z.at[d // 2],
                        (section, (f + d) % n),
                    )
                )
                onward[-1].start()
            else:
                sum_ref[...] = both
        for d, copy in zip(order, onward):
            copy.wait_recv()
            sum_ref[...] += far[d // 2].astype(jnp.float32)
        for copy in copies + onward:
            copy.wait_send()

    @pl.when(block != role)
    def _():
        partner = (2 * block + 1 - half, f)
        greet([partner])
        copy = remote(term_ref, other_ref, send_t.at[0], recv_t.at[0], partner)
        copy.start()
        copy.wait()


def hand_kernel(n, slices_ref, rows_ref, cols_ref, own_ref, send, recv, send_f):
    block, half, f = place()
    parts = n // 2
    piece = (f + 1) % n

    @pl.when(block == 0)
    def _():
        greet([(2 + half, parts * half + j) for j in range(parts)] + [(2 + half, f)])
        copies = []
        for j0 in range(parts):
            j = (j0 + f) % parts
            copies.append(
                remote(
                    slices_ref.at[j],
                    cols_ref.at[piece],
                    send.at[j0],
                    recv.at[piece],
                    (2 + half, parts * half + j),
                )
            )
        for copy in copies:
            copy.start()
        for copy in copies:
            copy.wait_send()
        copy = remote(rows_ref, own_ref, send.at[n], recv.at[n], (2 + half, f))
        copy.start()
        copy.wait_send()

    @pl.when(jnp.logical_and(block == 1, half == f // parts))
    def _():
        greet([(half, i) for i in range(n)] + [(half, f), (3 - half, f)])
        for p0 in range(n):
            p = (piece + p0) % n
            landed(cols_ref.at[p], recv.at[p])
            remote(cols_ref.at[p], cols_ref.at[p], send_f.at[p0], recv.at[p], (3 - half, f)).start()
        for p0 in range(n):
            p = (piece + p0) % n
            pltpu.make_async_copy(cols_ref.at[p], cols_ref.at[p], send_f.at[p0]).wait()
        landed(own_ref, recv.at[n])

    @pl.when(jnp.logical_and(block == 1, half != f // parts))
    def _():
        greet([(half, f), (3 - half, f)])
        for p in range(n):
            landed(cols_ref.at[p], recv.at[p])
        landed(own_ref, recv.at[n])


def return_kernel(n, grads_ref, full_ref, cols_ref, send, recv, send_z, send_f):
    block, half, f = place()
    parts = n // 2

    @pl.when(block == 1)
    def _():
        greet([(0, f), (1, f)])
        copy = remote(
            grads_ref.at[half],
            full_ref.at[half, f % parts],
            send.at[0],
            recv.at[2 * (f % parts) + half],
            (f // parts, f),
        )
        copy.start()
        copy.wait_send()
        copies = []
        for core in range(2):
            copies.append(
                remote(
                    grads_ref.at[half],
                    cols_ref.at[half],
                    send.at[1 + core],
                    recv.at[n + half],
                    (core, f),
                )
            )
        for copy in copies:
            copy.start()
        for copy in copies:
            copy.wait_send()

    @pl.when(block == 0)
    def _():
        line = [(half, (f + d) % n) for d in sorted(range(2, n, 2), key=lambda d: -min(d, n - d))]
        greet([(2, f), (3, f), (half, across(f))] + line)
        steps = parts // 2
        near = [f % 2 + 2 * ((i + f // 2) % steps) for i in range(steps)]
        far = [1 - f % 2 + 2 * ((i + f // 2) % steps) for i in range(steps)]
        copies = []
        for i, j in enumerate(near):
            for core in range(2):
                slot = full_ref.at[core, j]
                landed(slot, recv.at[2 * j + core])
                if i == 0:

                    @pl.when(parts * half + j == f)
                    def _():
                        for q, peer in enumerate(line):
                            remote(
                                slot, slot, send_z.at[2 * q + core], recv.at[2 * j + core], peer
                            ).start()

                copies.append(
                    remote(slot, slot, send_f.at[2 * i + core], recv.at[2 * j + core], (half, across(f)))
                )
                copies[-1].start()
        for core in range(2):
            landed(cols_ref.at[core], recv.at[n + core])
        for copy in copies:
            copy.wait_send()

        @pl.when(parts * half + near[0] == f)
        def _():
            for q in range(len(line)):
                for core in range(2):
                    slot = full_ref.at[core, near[0]]
                    pltpu.make_async_copy(slot, slot, send_z.at[2 * q + core]).wait()

        for j in far:
            for core in range(2):
                landed(full_ref.at[core, j], recv.at[2 * j + core])


def taps_kernel(samples, active_ref, out_ref):
    area = SIDE * SIDE
    lanes = active_ref.shape[1]
    col = lax.broadcasted_iota(jnp.int32, (area, lanes), 0) % SIDE
    for s in range(samples):
        base = s * area
        here = active_ref[base : base + area, :].astype(jnp.float32)
        before = jnp.where(col > 0, pltpu.roll(here, 1, 0), 0.0).astype(jnp.bfloat16)
        after = jnp.where(col < SIDE - 1, pltpu.roll(here, area - 1, 0), 0.0).astype(jnp.bfloat16)
        edge = jnp.zeros((SIDE, lanes), jnp.bfloat16)
        for c, value in enumerate((before, here.astype(jnp.bfloat16), after)):
            up = slice(c * lanes, (c + 1) * lanes)
            mid = slice((3 + c) * lanes, (4 + c) * lanes)
            down = slice((6 + c) * lanes, (7 + c) * lanes)
            out_ref[base + SIDE : base + area, up] = value[: area - SIDE]
            out_ref[base : base + SIDE, up] = edge
            out_ref[base : base + area, mid] = value
            out_ref[base : base + area - SIDE, down] = value[SIDE:]
            out_ref[base + area - SIDE : base + area, down] = edge


def conv_kernel(samples, active_ref, weight_ref, out_ref, taps):
    taps_kernel(samples, active_ref, taps)
    step = 256

    def chunk(i, carry):
        rows = pl.ds(pl.multiple_of(i * step, step), step)
        out_ref[rows, :] = jnp.dot(
            taps[rows, :], weight_ref[...], preferred_element_type=jnp.float32
        ).astype(out_ref.dtype)
        return carry

    lax.fori_loop(0, taps.shape[0] // step, chunk, 0)


def local(body, out, scratch, *args):
    return pl.pallas_call(
        body,
        out_shape=out,
        in_specs=[pl.BlockSpec(memory_space=pltpu.VMEM)] * len(args),
        out_specs=pl.BlockSpec(memory_space=pltpu.VMEM),
        scratch_shapes=scratch,
        compiler_params=pltpu.CompilerParams(vmem_limit_bytes=40 * 2**20),
    )(*args)


def weight_slope(samples, active_ref, slope_ref, grad_ref, taps):
    taps_kernel(samples, active_ref, taps)
    step = 3 * active_ref.shape[1]

    def chunk(i, carry):
        rows = pl.ds(pl.multiple_of(i * step, step), step)
        grad_ref[rows, :] = lax.dot_general(
            taps[:, rows], slope_ref[...], (((0,), (0,)), ((), ())), preferred_element_type=jnp.float32
        )
        return carry

    lax.fori_loop(0, 3, chunk, 0)


def collect_kernel(n, samples, grads_ref, active_ref, slope_ref, out_ref, grad_ref, taps, send, recv):
    block, half, f = place()
    parts = n // 2

    @pl.when(block == 0)
    def _():
        greet(
            [((half * n + f + d) % (2 * n) // n, (half * n + f + d) % (2 * n) % n) for d in range(1, 2 * n)]
        )
        mine = f % parts
        for q0 in range(parts):
            piece = half * parts + (q0 + f) % parts
            to = (piece + n - 1) % n
            own = jnp.logical_and(to == f, half == f // parts)

            @pl.when(jnp.logical_not(own))
            def _():
                remote(
                    grads_ref.at[piece], out_ref.at[mine], send.at[q0], recv.at[mine], (f // parts, to)
                ).start()

            @pl.when(own)
            def _():
                pltpu.make_async_copy(grads_ref.at[piece], out_ref.at[mine], recv.at[mine]).start()

    weight_slope(samples, active_ref, slope_ref, grad_ref, taps)

    @pl.when(block == 0)
    def _():
        for q0 in range(parts):
            piece = half * parts + (q0 + f) % parts
            own = jnp.logical_and((piece + n - 1) % n == f, half == f // parts)

            @pl.when(jnp.logical_not(own))
            def _():
                pltpu.make_async_copy(grads_ref.at[piece], grads_ref.at[piece], send.at[q0]).wait()

        for j in range(parts):
            landed(out_ref.at[j], recv.at[j])


def channel_split(signals, conv_weight, buckets):
    n = lax.axis_size("fsdp")
    tok, half = signals.shape
    chan = conv_weight.shape[0]
    parts = half // chan
    total = n * tok
    area = SIDE * SIDE
    samples = total // area
    group_width = 2 * half // GROUPS
    section = lax.axis_index("section")
    role_up = section >= 2
    f = lax.axis_index("fsdp")
    piece = (f + 1) % n
    bf16, f32 = jnp.bfloat16, jnp.float32

    live_h = jnp.repeat(16 + 2 * buckets[:, 0], samples // MICRO)
    live_w = jnp.repeat(16 + 2 * buckets[:, 1], samples // MICRO)
    cells = jnp.arange(SIDE)
    inside = (cells[None, :, None] < live_h[:, None, None]) & (cells[None, None, :] < live_w[:, None, None])
    mask = inside.astype(f32).reshape(samples, area, 1)
    mask_own = lax.dynamic_slice_in_dim(mask.reshape(total, 1), piece * tok, tok, axis=0)
    kcount = (live_h * live_w).astype(f32) * group_width

    def group_mean(value):
        columns = jnp.sum(value, axis=1)
        groups = jnp.sum(columns.reshape(samples, chan // group_width, group_width), axis=-1)
        return jnp.repeat(groups / kcount[:, None], group_width, axis=-1)[:, None, :]

    def normalize(values):
        masked = values * mask
        mean = group_mean(masked)
        spread = group_mean(masked * masked) - mean * mean
        scale = lax.rsqrt(spread + eps)
        normed = (values - mean) * scale
        return normed, scale, (mask * jax.nn.silu(normed)).astype(bf16)

    lanes = 128

    def padded(active):
        return jnp.pad(active.reshape(total, chan), ((0, 0), (0, lanes - chan)))

    wide = jnp.pad(conv_weight.transpose(1, 0, 2), ((0, 0), (0, lanes - chan), (0, 0))).reshape(9 * lanes, half)
    taps_scratch = pltpu.VMEM((total, 9 * lanes), bf16)

    def convolve(active):
        return local(
            functools.partial(conv_kernel, samples),
            jax.ShapeDtypeStruct((total, half), bf16),
            [taps_scratch],
            active,
            wide,
        ).reshape(n, tok, half)

    def convolve_back(slope):
        return (
            lax.conv_general_dilated(
                slope.reshape(samples, SIDE, SIDE, half),
                conv_weight[:, ::-1, :].transpose(1, 2, 0).reshape(3, 3, half, chan),
                (1, 1),
                "SAME",
                dimension_numbers=("NHWC", "HWIO", "NHWC"),
                preferred_element_type=f32,
            )
            .reshape(samples, area, chan)
            .astype(bf16)
        )

    def input_slope(term, other, normed, scale, grads):
        upstream = term.astype(f32) + other.astype(f32)
        gated = mask * upstream * silu_slope(normed)
        first = group_mean(gated)
        second = group_mean(gated * normed)
        return grads.astype(f32) + mask * (scale * (gated - first - normed * second))

    def sliced(rows):
        return rows.reshape(tok, parts, chan).transpose(1, 0, 2)

    whole = (samples, area, chan)
    cols, full = communicate(
        functools.partial(spread_kernel, n),
        0,
        (signals, sliced(signals)),
        [((n, tok, chan), bf16), ((n, tok, half), bf16)],
        (parts, n, n, n, n),
    )
    cols = cols.reshape(whole)

    values = (cols.astype(f32) * mask).astype(bf16).astype(f32)
    normed_down, scale_down, active_down = normalize(values)
    active_down = padded(active_down)

    def first_down():
        return convolve(active_down), jnp.zeros(whole, bf16)

    def first_up():
        slope = (full.reshape(samples, area, half).astype(f32) * mask).astype(bf16)
        return jnp.zeros((n, tok, half), bf16), convolve_back(slope)

    mixed, term = lax.cond(role_up, first_up, first_down)
    partial_rows, other = communicate(
        functools.partial(reduce_kernel, n, 0),
        1,
        (mixed, term),
        [((tok, half), f32), (whole, bf16)],
        (parts, parts, parts, parts, 1, 1),
        [pltpu.VMEM((parts, tok, half), bf16)] * 3,
        (0, 2),
    )

    def block_rows(rows, pieces):
        return (rows + mask_own * pieces).astype(bf16)

    start_rows = (signals.astype(f32) * mask_own).astype(bf16).astype(f32)
    handed = block_rows(start_rows, partial_rows)
    skip_cols, skip_rows = communicate(
        functools.partial(hand_kernel, n),
        2,
        (sliced(handed), handed),
        [((n, tok, chan), bf16), ((tok, half), bf16)],
        (n + 1, n + 1, n),
    )

    def second_up():
        normed, scale, active = normalize(skip_cols.reshape(whole).astype(f32))
        slope = mask * input_slope(term, other, normed, scale, cols)
        return slope.astype(bf16), padded(active)

    def second_down():
        return jnp.zeros(whole, bf16), active_down

    grads, active = lax.cond(role_up, second_up, second_down)
    back, back_cols = communicate(
        functools.partial(return_kernel, n),
        3,
        (grads.reshape(2, total // 2, chan).transpose(0, 2, 1),),
        [((2, parts, chan, total // 2), bf16), ((2, chan, total // 2), bf16)],
        (3, n + 2, n, parts),
    )

    def third_up():
        slope = (full.reshape(samples, area, half).astype(f32) * mask).astype(bf16)
        return convolve(active), jnp.zeros(whole, bf16), slope.reshape(total, half)

    def third_down():
        slope = back.reshape(2, half, total // 2).transpose(0, 2, 1).reshape(total, half)
        return jnp.zeros((n, tok, half), bf16), convolve_back(slope), slope

    mixed, term, slope = lax.cond(role_up, third_up, third_down)
    partial_rows, other = communicate(
        functools.partial(reduce_kernel, n, 1),
        4,
        (mixed, term),
        [((tok, half), f32), (whole, bf16)],
        (parts, parts, parts, parts, 1, 1),
        [pltpu.VMEM((parts, tok, half), bf16)] * 3,
        (0, 2),
    )

    def last_down():
        slope = input_slope(term, other, normed_down, scale_down, back_cols.transpose(0, 2, 1).reshape(whole))
        return (mask * slope).astype(bf16)

    def last_up():
        return jnp.zeros(whole, bf16)

    grads = lax.cond(role_up, last_up, last_down)
    pieces, grad_weight = communicate(
        functools.partial(collect_kernel, n, samples),
        5,
        (grads.reshape(n, tok, chan), active, slope),
        [((parts, tok, chan), bf16), ((9 * lanes, half), f32)],
        (parts, parts),
        [taps_scratch],
        (1, 2, 4),
    )
    grad_weight = grad_weight.reshape(9, lanes, half)[:, :chan].transpose(1, 0, 2)
    down_rows = pieces.transpose(1, 0, 2).reshape(tok, half)
    results = jnp.where(role_up, block_rows(skip_rows.astype(f32), partial_rows), down_rows)
    return results, grad_weight


def per_device(signals, conv_weight, buckets):
    n = lax.axis_size("fsdp")
    chan = conv_weight.shape[0]
    half = signals.shape[1]
    fits = (
        lax.axis_size("section") == 4
        and n % 4 == 0
        and chan <= 128
        and chan % (2 * half // GROUPS) == 0
        and half == chan * (n // 2)
        and n * signals.shape[0] == MICRO * SIDE * SIDE
    )
    return (channel_split if fits else general)(signals, conv_weight, buckets)


def solution(mesh):
    return jax.shard_map(
        per_device,
        mesh=mesh,
        in_specs=(P("fsdp", "section"), P("fsdp", None, "section"), P()),
        out_specs=(P("fsdp", "section"), P("fsdp", None, "section")),
        check_vma=False,
    )
```

```python
import functools

import jax
import jax.numpy as jnp
from jax import lax
from jax.experimental import pallas as pl
from jax.experimental.pallas import tpu as pltpu
from jax.sharding import PartitionSpec as P

GROUPS = 32
SIDE = 32
MICRO = 2
ROWS_DEV = 8


eps = 1e-05


def from_partner(value, axis, stride):
    mask = 2**stride
    pairs = [(source, source ^ mask) for source in range(lax.axis_size(axis))]
    return lax.ppermute(value, axis, pairs)


def padded_2(cells, sides, width):
    for axis, dim in sides:
        count = lax.axis_size(axis)
        head = lax.slice_in_dim(cells, 0, width, axis=dim)
        tail = lax.slice_in_dim(cells, cells.shape[dim] - width, cells.shape[dim], axis=dim)
        cells = jnp.concatenate(
            [
                lax.ppermute(tail, axis, [(i, (i + 1) % count) for i in range(count)]),
                cells,
                lax.ppermute(head, axis, [((i + 1) % count, i) for i in range(count)]),
            ],
            axis=dim,
        )
    return cells


def silu_slope(value):
    sig = jax.nn.sigmoid(value)
    return sig * (1.0 + value * (1.0 - sig))


def section_swap(value, bit):
    return from_partner(value, "section", bit)


def general(signals, conv_weight, buckets):
    tok = signals.shape[0]
    half = signals.shape[1]
    width = 2 * half
    group_width = width // GROUPS
    local_groups = half // group_width
    section_index = lax.axis_index("section")
    upper_half = section_index % 2 == 1
    role_up = section_index >= 2
    fsdp_index = lax.axis_index("fsdp")
    pieces = SIDE // ROWS_DEV
    samples = lax.axis_size("fsdp") // pieces
    shifted = fsdp_index + 1
    sample_id = shifted // pieces % samples
    piece_id = shifted % pieces
    micro_id = sample_id // (samples // MICRO)
    picked_micro = jnp.arange(MICRO) == micro_id
    bucket_h = jnp.sum(jnp.where(picked_micro, buckets[:, 0], 0))
    bucket_w = jnp.sum(jnp.where(picked_micro, buckets[:, 1], 0))
    live_h = 16 + 2 * bucket_h
    live_w = 16 + 2 * bucket_w
    row_ids = piece_id * ROWS_DEV + jnp.arange(ROWS_DEV)
    col_ids = jnp.arange(SIDE)
    mask_grid = ((row_ids[:, None] < live_h) & (col_ids[None, :] < live_w)).astype(jnp.float32)
    mask_flat = mask_grid.reshape(tok, 1)
    group_count = (live_h * live_w).astype(jnp.float32) * group_width
    sample_hot = (jnp.arange(samples) == sample_id).astype(jnp.float32)[:, None]

    def with_rims(field):
        grid = field.reshape(ROWS_DEV, SIDE, field.shape[-1])
        padded = padded_2(grid, (("fsdp", 0),), 1)
        top = jnp.where(piece_id > 0, padded[:1], jnp.zeros_like(padded[:1]))
        bottom = jnp.where(piece_id < pieces - 1, padded[-1:], jnp.zeros_like(padded[-1:]))
        padded = jnp.concatenate([top, padded[1:-1], bottom], axis=0)
        return jnp.pad(padded, ((0, 0), (1, 1), (0, 0)))

    def group_totals(first, second):
        total_first, total_second = lax.psum(
            (sample_hot * first[None, :], sample_hot * second[None, :]), "fsdp"
        )
        return (
            jnp.sum(sample_hot * total_first, axis=0),
            jnp.sum(sample_hot * total_second, axis=0),
        )

    def normalize(values):
        grouped = values.reshape(tok, local_groups, group_width)
        masked = grouped * mask_flat[:, :, None]
        first = jnp.sum(masked, axis=(0, 2))
        second = jnp.sum(masked * masked, axis=(0, 2))
        total_first, total_second = group_totals(first, second)
        mean = total_first / group_count
        spread = total_second / group_count - mean * mean
        scale = lax.rsqrt(spread + eps)
        normed = (grouped - mean[None, :, None]) * scale[None, :, None]
        return (normed.reshape(tok, half), scale)

    def forward(inputs, weights):
        values = inputs.astype(jnp.float32)
        normed, scale = normalize(values)
        activated = (mask_flat * jax.nn.silu(normed)).astype(jnp.bfloat16)
        padded = with_rims(activated)
        partner = section_swap(padded, 0)
        lower = jnp.where(upper_half, partner, padded)
        upper = jnp.where(upper_half, padded, partner)
        full = jnp.concatenate([lower, upper], axis=-1)
        mixed = jnp.zeros((tok, half), jnp.float32)
        for tap in range(9):
            row_off, col_off = (tap // 3, tap % 3)
            slab = full[row_off : row_off + ROWS_DEV, col_off : col_off + SIDE].reshape(tok, width)
            mixed = mixed + jnp.dot(slab, weights[:, tap, :], preferred_element_type=jnp.float32)
        output = (values + mask_flat * mixed).astype(jnp.bfloat16)
        return (output, (normed, scale, full))

    def backward(grads, cache, weights):
        normed, scale, full = cache
        slope = (grads.astype(jnp.float32) * mask_flat).astype(jnp.bfloat16)
        padded = with_rims(slope)
        partial_value = jnp.zeros((tok, width), jnp.float32)
        for tap in range(9):
            row_off, col_off = (tap // 3, tap % 3)
            slab = padded[
                2 - row_off : 2 - row_off + ROWS_DEV, 2 - col_off : 2 - col_off + SIDE
            ].reshape(tok, half)
            partial_value = partial_value + lax.dot_general(
                slab,
                weights[:, tap, :],
                (((1,), (1,)), ((), ())),
                preferred_element_type=jnp.float32,
            )
        keep = jnp.where(upper_half, partial_value[:, half:], partial_value[:, :half])
        send = jnp.where(upper_half, partial_value[:, :half], partial_value[:, half:]).astype(
            jnp.bfloat16
        )
        arrived = section_swap(send, 0)
        kept = lax.optimization_barrier(keep.astype(jnp.bfloat16)).astype(jnp.float32)
        upstream = kept + arrived.astype(jnp.float32)
        gated = mask_flat * upstream * silu_slope(normed)
        grouped = gated.reshape(tok, local_groups, group_width)
        normed_grouped = normed.reshape(tok, local_groups, group_width)
        first = jnp.sum(grouped, axis=(0, 2))
        second = jnp.sum(grouped * normed_grouped, axis=(0, 2))
        total_first, total_second = group_totals(first, second)
        centred = (
            grouped
            - (total_first / group_count)[None, :, None]
            - normed_grouped * (total_second / group_count)[None, :, None]
        )
        through = mask_flat * (scale[None, :, None] * centred).reshape(tok, half)
        return (grads.astype(jnp.float32) + through, slope)

    weights = lax.all_gather(conv_weight, "fsdp", axis=0, tiled=True)
    start = (signals.astype(jnp.float32) * mask_flat).astype(jnp.bfloat16)
    first_out, first_cache = forward(start, weights)
    handed = section_swap(first_out, 1)
    second_out, second_cache = forward(handed, weights)
    back_weights = lax.all_gather(conv_weight, "fsdp", axis=0, tiled=True)
    up_grads, up_slope = backward(signals, second_cache, back_weights)
    returned = section_swap(up_grads.astype(jnp.bfloat16), 1)
    down_grads, down_slope = backward(returned, first_cache, back_weights)
    results = jnp.where(role_up, second_out, (mask_flat * down_grads).astype(jnp.bfloat16))
    chosen_full = jnp.where(role_up, second_cache[2], first_cache[2])
    chosen_slope = jnp.where(role_up, up_slope, down_slope)
    taps = []
    for tap in range(9):
        row_off, col_off = (tap // 3, tap % 3)
        slab = chosen_full[row_off : row_off + ROWS_DEV, col_off : col_off + SIDE].reshape(
            tok, width
        )
        taps.append(
            lax.dot_general(
                slab, chosen_slope, (((0,), (0,)), ((), ())), preferred_element_type=jnp.float32
            )
        )
    grad_weight = lax.psum_scatter(jnp.stack(taps, axis=1), "fsdp", scatter_dimension=0, tiled=True)
    return (results, grad_weight)


MESH = pl.DeviceIdType.MESH


def place():
    section = lax.axis_index("section")
    return section // 2, section % 2, lax.axis_index("fsdp")


def greet(peers):
    barrier = pltpu.get_barrier_semaphore()
    for peer in peers:
        pl.semaphore_signal(barrier, inc=1, device_id=peer, device_id_type=MESH)
    pl.semaphore_wait(barrier, len(peers))


def remote(src, dst, send, recv, peer):
    return pltpu.make_async_remote_copy(
        src_ref=src, dst_ref=dst, send_sem=send, recv_sem=recv, device_id=peer, device_id_type=MESH
    )


def landed(dst, sem):
    pltpu.make_async_copy(dst, dst, sem).wait()


def communicate(body, cid, args, outs, sems, scratch=(), fast=()):
    spaces = [pltpu.VMEM if i in fast else pl.ANY for i in range(len(args) + len(outs))]
    specs = [pl.BlockSpec(memory_space=space) for space in spaces]
    return pl.pallas_call(
        body,
        out_shape=[jax.ShapeDtypeStruct(shape, dtype) for shape, dtype in outs],
        in_specs=specs[: len(args)],
        out_specs=specs[len(args) :],
        scratch_shapes=list(scratch) + [pltpu.SemaphoreType.DMA((count,)) for count in sems],
        compiler_params=pltpu.CompilerParams(
            collective_id=cid, has_side_effects=True, vmem_limit_bytes=40 * 2**20
        ),
    )(*args)


def across(f):
    return f + 1 - 2 * (f % 2)


def spread_kernel(n, rows_ref, slices_ref, cols_ref, full_ref, send_a, send_f, recv_a, send_g, recv_g):
    block, half, f = place()
    parts = n // 2
    piece = (f + 1) % n
    peers = []
    for d in range(1, 2 * n):
        other = (half * n + f + d) % (2 * n)
        peers.append((2 * block + other // n, other % n))
    greet(peers)
    for j0 in range(parts):
        j = (j0 + f) % parts
        to = parts * half + j

        @pl.when(to != f)
        def _():
            remote(
                slices_ref.at[j], cols_ref.at[piece], send_a.at[j0], recv_a.at[piece], (2 * block + half, to)
            ).start()

        @pl.when(to == f)
        def _():
            pltpu.make_async_copy(slices_ref.at[j], cols_ref.at[piece], recv_a.at[piece]).start()

    @pl.when(block == 1)
    def _():
        pltpu.make_async_copy(rows_ref, full_ref.at[piece], recv_g.at[piece]).start()
        for d in range(2, n, 2):
            remote(
                rows_ref, full_ref.at[piece], send_g.at[d], recv_g.at[piece], (2 + half, (f + d) % n)
            ).start()
        remote(rows_ref, full_ref.at[piece], send_g.at[0], recv_g.at[piece], (2 + half, across(f))).start()

    @pl.when(block == 1)
    def _():
        for d in range(2, n, 2):
            p = (piece + d) % n
            landed(full_ref.at[p], recv_g.at[p])
            remote(
                full_ref.at[p], full_ref.at[p], send_g.at[d + 1], recv_g.at[p], (2 + half, across(f))
            ).start()

    @pl.when(half == f // parts)
    def _():
        for p0 in range(n):
            p = (piece + p0) % n
            landed(cols_ref.at[p], recv_a.at[p])
            remote(
                cols_ref.at[p], cols_ref.at[p], send_f.at[p0], recv_a.at[p], (2 * block + 1 - half, f)
            ).start()
        for p0 in range(n):
            p = (piece + p0) % n
            pltpu.make_async_copy(cols_ref.at[p], cols_ref.at[p], send_f.at[p0]).wait()

    @pl.when(half != f // parts)
    def _():
        for p in range(n):
            landed(cols_ref.at[p], recv_a.at[p])

    @pl.when(block == 1)
    def _():
        for d in range(0, n, 2):
            pltpu.make_async_copy(rows_ref, rows_ref, send_g.at[d]).wait()
        for d in range(2, n, 2):
            p = (piece + d) % n
            pltpu.make_async_copy(full_ref.at[p], full_ref.at[p], send_g.at[d + 1]).wait()
        landed(full_ref.at[piece], recv_g.at[piece])
        for d in range(0, n, 2):
            p = (across(f) + 1 + d) % n
            landed(full_ref.at[p], recv_g.at[p])

    for j0 in range(parts):
        j = (j0 + f) % parts

        @pl.when(parts * half + j != f)
        def _():
            pltpu.make_async_copy(slices_ref.at[j], slices_ref.at[j], send_a.at[j0]).wait()


def reduce_kernel(
    n, role, mixed_ref, term_ref, sum_ref, other_ref, near, pair, far, send, recv, send_z, recv_z, send_t, recv_t
):
    block, half, f = place()

    @pl.when(block == role)
    def _():
        section = 2 * block + half
        greet([(section, across(f))] + [(section, (f + d) % n) for d in range(2, n, 2)])
        order = sorted(range(0, n, 2), key=lambda d: -min(d, n - d))
        copies = []
        for d in order:
            to = (across(f) + d) % n
            copies.append(
                remote(
                    mixed_ref.at[(to + 1) % n],
                    near.at[d // 2],
                    send.at[d // 2],
                    recv.at[d // 2],
                    (section, across(f)),
                )
            )
            copies[-1].start()
        onward = []
        for d, copy in zip(order, copies):
            copy.wait_recv()
            both = mixed_ref[(f + d + 1) % n].astype(jnp.float32) + near[d // 2].astype(jnp.float32)
            if d:
                pair[d // 2] = both.astype(jnp.bfloat16)
                onward.append(
                    remote(
                        pair.at[d // 2],
                        far.at[d // 2],
                        send_z.at[d // 2],
                        recv_z.at[d // 2],
                        (section, (f + d) % n),
                    )
                )
                onward[-1].start()
            else:
                sum_ref[...] = both
        for d, copy in zip(order, onward):
            copy.wait_recv()
            sum_ref[...] += far[d // 2].astype(jnp.float32)
        for copy in copies + onward:
            copy.wait_send()

    @pl.when(block != role)
    def _():
        partner = (2 * block + 1 - half, f)
        greet([partner])
        copy = remote(term_ref, other_ref, send_t.at[0], recv_t.at[0], partner)
        copy.start()
        copy.wait()


def hand_kernel(n, slices_ref, rows_ref, cols_ref, own_ref, send, recv, send_f):
    block, half, f = place()
    parts = n // 2
    piece = (f + 1) % n

    @pl.when(block == 0)
    def _():
        greet([(2 + half, parts * half + j) for j in range(parts)] + [(2 + half, f)])
        copies = []
        for j0 in range(parts):
            j = (j0 + f) % parts
            copies.append(
                remote(
                    slices_ref.at[j],
                    cols_ref.at[piece],
                    send.at[j0],
                    recv.at[piece],
                    (2 + half, parts * half + j),
                )
            )
        for copy in copies:
            copy.start()
        for copy in copies:
            copy.wait_send()
        copy = remote(rows_ref, own_ref, send.at[n], recv.at[n], (2 + half, f))
        copy.start()
        copy.wait_send()

    @pl.when(jnp.logical_and(block == 1, half == f // parts))
    def _():
        greet([(half, i) for i in range(n)] + [(half, f), (3 - half, f)])
        for p0 in range(n):
            p = (piece + p0) % n
            landed(cols_ref.at[p], recv.at[p])
            remote(cols_ref.at[p], cols_ref.at[p], send_f.at[p0], recv.at[p], (3 - half, f)).start()
        for p0 in range(n):
            p = (piece + p0) % n
            pltpu.make_async_copy(cols_ref.at[p], cols_ref.at[p], send_f.at[p0]).wait()
        landed(own_ref, recv.at[n])

    @pl.when(jnp.logical_and(block == 1, half != f // parts))
    def _():
        greet([(half, f), (3 - half, f)])
        for p in range(n):
            landed(cols_ref.at[p], recv.at[p])
        landed(own_ref, recv.at[n])


def return_kernel(n, grads_ref, full_ref, cols_ref, send, recv, send_z, send_f):
    block, half, f = place()
    parts = n // 2

    @pl.when(block == 1)
    def _():
        greet([(0, f), (1, f)])
        copy = remote(
            grads_ref.at[half],
            full_ref.at[half, f % parts],
            send.at[0],
            recv.at[2 * (f % parts) + half],
            (f // parts, f),
        )
        copy.start()
        copy.wait_send()
        copies = []
        for core in range(2):
            copies.append(
                remote(
                    grads_ref.at[half],
                    cols_ref.at[half],
                    send.at[1 + core],
                    recv.at[n + half],
                    (core, f),
                )
            )
        for copy in copies:
            copy.start()
        for copy in copies:
            copy.wait_send()

    @pl.when(block == 0)
    def _():
        line = [(half, (f + d) % n) for d in sorted(range(2, n, 2), key=lambda d: -min(d, n - d))]
        greet([(2, f), (3, f), (half, across(f))] + line)
        steps = parts // 2
        near = [f % 2 + 2 * ((i + f // 2) % steps) for i in range(steps)]
        far = [1 - f % 2 + 2 * ((i + f // 2) % steps) for i in range(steps)]
        copies = []
        for i, j in enumerate(near):
            for core in range(2):
                slot = full_ref.at[core, j]
                landed(slot, recv.at[2 * j + core])
                if i == 0:

                    @pl.when(parts * half + j == f)
                    def _():
                        for q, peer in enumerate(line):
                            remote(
                                slot, slot, send_z.at[2 * q + core], recv.at[2 * j + core], peer
                            ).start()

                copies.append(
                    remote(slot, slot, send_f.at[2 * i + core], recv.at[2 * j + core], (half, across(f)))
                )
                copies[-1].start()
        for core in range(2):
            landed(cols_ref.at[core], recv.at[n + core])
        for copy in copies:
            copy.wait_send()

        @pl.when(parts * half + near[0] == f)
        def _():
            for q in range(len(line)):
                for core in range(2):
                    slot = full_ref.at[core, near[0]]
                    pltpu.make_async_copy(slot, slot, send_z.at[2 * q + core]).wait()

        for j in far:
            for core in range(2):
                landed(full_ref.at[core, j], recv.at[2 * j + core])


def taps_kernel(samples, active_ref, out_ref):
    area = SIDE * SIDE
    lanes = active_ref.shape[1]
    col = lax.broadcasted_iota(jnp.int32, (area, lanes), 0) % SIDE
    for s in range(samples):
        base = s * area
        here = active_ref[base : base + area, :].astype(jnp.float32)
        before = jnp.where(col > 0, pltpu.roll(here, 1, 0), 0.0).astype(jnp.bfloat16)
        after = jnp.where(col < SIDE - 1, pltpu.roll(here, area - 1, 0), 0.0).astype(jnp.bfloat16)
        edge = jnp.zeros((SIDE, lanes), jnp.bfloat16)
        for c, value in enumerate((before, here.astype(jnp.bfloat16), after)):
            up = slice(c * lanes, (c + 1) * lanes)
            mid = slice((3 + c) * lanes, (4 + c) * lanes)
            down = slice((6 + c) * lanes, (7 + c) * lanes)
            out_ref[base + SIDE : base + area, up] = value[: area - SIDE]
            out_ref[base : base + SIDE, up] = edge
            out_ref[base : base + area, mid] = value
            out_ref[base : base + area - SIDE, down] = value[SIDE:]
            out_ref[base + area - SIDE : base + area, down] = edge


def copy_kernel(in_ref, out_ref):
    out_ref[...] = in_ref[...]


def conv_kernel(samples, active_ref, weight_ref, out_ref, taps):
    taps_kernel(samples, active_ref, taps)
    step = 256

    def chunk(i, carry):
        rows = pl.ds(pl.multiple_of(i * step, step), step)
        out_ref[rows, :] = jnp.dot(
            taps[rows, :], weight_ref[...], preferred_element_type=jnp.float32
        ).astype(out_ref.dtype)
        return carry

    lax.fori_loop(0, taps.shape[0] // step, chunk, 0)


def local(body, out, scratch, *args):
    return pl.pallas_call(
        body,
        out_shape=out,
        in_specs=[pl.BlockSpec(memory_space=pltpu.VMEM)] * len(args),
        out_specs=pl.BlockSpec(memory_space=pltpu.VMEM),
        scratch_shapes=scratch,
        compiler_params=pltpu.CompilerParams(vmem_limit_bytes=40 * 2**20),
    )(*args)


def weight_slope(samples, active_ref, slope_ref, grad_ref, taps):
    taps_kernel(samples, active_ref, taps)
    step = 3 * active_ref.shape[1]

    def chunk(i, carry):
        rows = pl.ds(pl.multiple_of(i * step, step), step)
        grad_ref[rows, :] = lax.dot_general(
            taps[:, rows], slope_ref[...], (((0,), (0,)), ((), ())), preferred_element_type=jnp.float32
        )
        return carry

    lax.fori_loop(0, 3, chunk, 0)


def collect_kernel(n, samples, grads_ref, active_ref, slope_ref, out_ref, grad_ref, taps, send, recv):
    block, half, f = place()
    parts = n // 2

    @pl.when(block == 0)
    def _():
        greet(
            [((half * n + f + d) % (2 * n) // n, (half * n + f + d) % (2 * n) % n) for d in range(1, 2 * n)]
        )
        mine = f % parts
        for q0 in range(parts):
            piece = half * parts + (q0 + f) % parts
            to = (piece + n - 1) % n
            own = jnp.logical_and(to == f, half == f // parts)

            @pl.when(jnp.logical_not(own))
            def _():
                remote(
                    grads_ref.at[piece], out_ref.at[mine], send.at[q0], recv.at[mine], (f // parts, to)
                ).start()

            @pl.when(own)
            def _():
                pltpu.make_async_copy(grads_ref.at[piece], out_ref.at[mine], recv.at[mine]).start()

    weight_slope(samples, active_ref, slope_ref, grad_ref, taps)

    @pl.when(block == 0)
    def _():
        for q0 in range(parts):
            piece = half * parts + (q0 + f) % parts
            own = jnp.logical_and((piece + n - 1) % n == f, half == f // parts)

            @pl.when(jnp.logical_not(own))
            def _():
                pltpu.make_async_copy(grads_ref.at[piece], grads_ref.at[piece], send.at[q0]).wait()

        for j in range(parts):
            landed(out_ref.at[j], recv.at[j])


def channel_split(signals, conv_weight, buckets):
    n = lax.axis_size("fsdp")
    tok, half = signals.shape
    chan = conv_weight.shape[0]
    parts = half // chan
    total = n * tok
    area = SIDE * SIDE
    samples = total // area
    group_width = 2 * half // GROUPS
    section = lax.axis_index("section")
    role_up = section >= 2
    f = lax.axis_index("fsdp")
    piece = (f + 1) % n
    bf16, f32 = jnp.bfloat16, jnp.float32

    live_h = jnp.repeat(16 + 2 * buckets[:, 0], samples // MICRO)
    live_w = jnp.repeat(16 + 2 * buckets[:, 1], samples // MICRO)
    cells = jnp.arange(SIDE)
    inside = (cells[None, :, None] < live_h[:, None, None]) & (cells[None, None, :] < live_w[:, None, None])
    mask = inside.astype(f32).reshape(samples, area, 1)
    mask_own = lax.dynamic_slice_in_dim(mask.reshape(total, 1), piece * tok, tok, axis=0)
    kcount = (live_h * live_w).astype(f32) * group_width

    def group_mean(value):
        columns = jnp.sum(value, axis=1)
        groups = jnp.sum(columns.reshape(samples, chan // group_width, group_width), axis=-1)
        return jnp.repeat(groups / kcount[:, None], group_width, axis=-1)[:, None, :]

    def normalize(values):
        masked = values * mask
        mean = group_mean(masked)
        spread = group_mean(masked * masked) - mean * mean
        scale = lax.rsqrt(spread + eps)
        normed = (values - mean) * scale
        return normed, scale, (mask * jax.nn.silu(normed)).astype(bf16)

    lanes = 128

    def padded(active):
        out = jax.ShapeDtypeStruct((total, lanes), bf16)
        return local(copy_kernel, out, [], jnp.pad(active.reshape(total, chan), ((0, 0), (0, lanes - chan))))

    wide = jnp.pad(conv_weight.transpose(1, 0, 2), ((0, 0), (0, lanes - chan), (0, 0))).reshape(9 * lanes, half)
    taps_scratch = pltpu.VMEM((total, 9 * lanes), bf16)

    def convolve(active):
        return local(
            functools.partial(conv_kernel, samples),
            jax.ShapeDtypeStruct((total, half), bf16),
            [taps_scratch],
            active,
            wide,
        ).reshape(n, tok, half)

    def convolve_back(slope):
        return (
            lax.conv_general_dilated(
                slope.reshape(samples, SIDE, SIDE, half),
                conv_weight[:, ::-1, :].transpose(1, 2, 0).reshape(3, 3, half, chan),
                (1, 1),
                "SAME",
                dimension_numbers=("NHWC", "HWIO", "NHWC"),
                preferred_element_type=f32,
            )
            .reshape(samples, area, chan)
            .astype(bf16)
        )

    def input_slope(term, other, normed, scale, grads):
        upstream = term.astype(f32) + other.astype(f32)
        gated = mask * upstream * silu_slope(normed)
        first = group_mean(gated)
        second = group_mean(gated * normed)
        return grads.astype(f32) + mask * (scale * (gated - first - normed * second))

    def sliced(rows):
        return rows.reshape(tok, parts, chan).transpose(1, 0, 2)

    whole = (samples, area, chan)
    cols, full = communicate(
        functools.partial(spread_kernel, n),
        0,
        (signals, sliced(signals)),
        [((n, tok, chan), bf16), ((n, tok, half), bf16)],
        (parts, n, n, n, n),
    )
    cols = cols.reshape(whole)

    values = (cols.astype(f32) * mask).astype(bf16).astype(f32)
    normed_down, scale_down, active_down = normalize(values)
    active_down = padded(active_down)

    def first_down():
        return convolve(active_down), jnp.zeros(whole, bf16)

    def first_up():
        slope = (full.reshape(samples, area, half).astype(f32) * mask).astype(bf16)
        return jnp.zeros((n, tok, half), bf16), convolve_back(slope)

    mixed, term = lax.cond(role_up, first_up, first_down)
    partial_rows, other = communicate(
        functools.partial(reduce_kernel, n, 0),
        1,
        (mixed, term),
        [((tok, half), f32), (whole, bf16)],
        (parts, parts, parts, parts, 1, 1),
        [pltpu.VMEM((parts, tok, half), bf16)] * 3,
        (0, 2),
    )

    def block_rows(rows, pieces):
        return (rows + mask_own * pieces).astype(bf16)

    start_rows = (signals.astype(f32) * mask_own).astype(bf16).astype(f32)
    handed = block_rows(start_rows, partial_rows)
    skip_cols, skip_rows = communicate(
        functools.partial(hand_kernel, n),
        2,
        (sliced(handed), handed),
        [((n, tok, chan), bf16), ((tok, half), bf16)],
        (n + 1, n + 1, n),
    )

    def second_up():
        normed, scale, active = normalize(skip_cols.reshape(whole).astype(f32))
        slope = mask * input_slope(term, other, normed, scale, cols)
        return slope.astype(bf16), padded(active)

    def second_down():
        return jnp.zeros(whole, bf16), active_down

    grads, active = lax.cond(role_up, second_up, second_down)
    back, back_cols = communicate(
        functools.partial(return_kernel, n),
        3,
        (grads.reshape(2, total // 2, chan).transpose(0, 2, 1),),
        [((2, parts, chan, total // 2), bf16), ((2, chan, total // 2), bf16)],
        (3, n + 2, n, parts),
    )

    def third_up():
        slope = (full.reshape(samples, area, half).astype(f32) * mask).astype(bf16)
        return convolve(active), jnp.zeros(whole, bf16), slope.reshape(total, half)

    def third_down():
        slope = back.reshape(2, half, total // 2).transpose(0, 2, 1).reshape(total, half)
        return jnp.zeros((n, tok, half), bf16), convolve_back(slope), slope

    mixed, term, slope = lax.cond(role_up, third_up, third_down)
    partial_rows, other = communicate(
        functools.partial(reduce_kernel, n, 1),
        4,
        (mixed, term),
        [((tok, half), f32), (whole, bf16)],
        (parts, parts, parts, parts, 1, 1),
        [pltpu.VMEM((parts, tok, half), bf16)] * 3,
        (0, 2),
    )

    def last_down():
        slope = input_slope(term, other, normed_down, scale_down, back_cols.transpose(0, 2, 1).reshape(whole))
        return (mask * slope).astype(bf16)

    def last_up():
        return jnp.zeros(whole, bf16)

    grads = lax.cond(role_up, last_up, last_down)
    pieces, grad_weight = communicate(
        functools.partial(collect_kernel, n, samples),
        5,
        (grads.reshape(n, tok, chan), active, slope),
        [((parts, tok, chan), bf16), ((9 * lanes, half), f32)],
        (parts, parts),
        [taps_scratch],
        (1, 2, 4),
    )
    grad_weight = grad_weight.reshape(9, lanes, half)[:, :chan].transpose(1, 0, 2)
    down_rows = pieces.transpose(1, 0, 2).reshape(tok, half)
    results = jnp.where(role_up, block_rows(skip_rows.astype(f32), partial_rows), down_rows)
    return results, grad_weight


def per_device(signals, conv_weight, buckets):
    n = lax.axis_size("fsdp")
    chan = conv_weight.shape[0]
    half = signals.shape[1]
    fits = (
        lax.axis_size("section") == 4
        and n % 4 == 0
        and chan <= 128
        and chan % (2 * half // GROUPS) == 0
        and half == chan * (n // 2)
        and n * signals.shape[0] == MICRO * SIDE * SIDE
    )
    return (channel_split if fits else general)(signals, conv_weight, buckets)


def solution(mesh):
    return jax.shard_map(
        per_device,
        mesh=mesh,
        in_specs=(P("fsdp", "section"), P("fsdp", None, "section"), P()),
        out_specs=(P("fsdp", "section"), P("fsdp", None, "section")),
        check_vma=False,
    )
```
